32 devices in a mesh: shard: 4 (over z), ctx: 2 (over x), tp: 4 (over y, core).
Axes of the slice: x: 2, y: 2, z: 4, core: 2. Of those that a mesh axis runs over, the one named last changes fastest.
Arguments:
- inputs: bfloat16 [4, 2048, 1024], P('shard', ('ctx', 'tp')), may hold values from -6 to 6
- encoded: bfloat16 [4, 512, 1024], P('shard', 'ctx'), may hold values from -6 to 6
- doc_lengths: int32 [4, 4], P('shard'), may hold values from 1 to 1025, 2048 in all within a row
- cotangent: bfloat16 [4, 2048, 1024], P('shard', ('ctx', 'tp')), may hold values from -6 to 6
- query_weight: bfloat16 [1024, 1024], P('shard', 'tp'), may hold values from -0.1875 to 0.1875
- key_weight: bfloat16 [1024, 1024], P('shard', 'tp'), may hold values from -0.1875 to 0.1875
- value_weight: bfloat16 [1024, 1024], P('shard', 'tp'), may hold values from -0.1875 to 0.1875
- out_weight: bfloat16 [1024, 1024], P('tp', 'shard'), may hold values from -3 to 3
- memory_query: bfloat16 [1024, 1024], P('shard', 'tp'), may hold values from -0.1875 to 0.1875
- memory_key: bfloat16 [1024, 1024], P('shard', 'tp'), may hold values from -0.1875 to 0.1875
- memory_value: bfloat16 [1024, 1024], P('shard', 'tp'), may hold values from -0.1875 to 0.1875
- memory_out: bfloat16 [1024, 1024], P('tp', 'shard'), may hold values from -4 to 4
- up_weight: bfloat16 [1024, 4096], P('shard', 'tp'), may hold values from -0.1875 to 0.1875
- down_weight: bfloat16 [4096, 1024], P('tp', 'shard'), may hold values from -0.09375 to 0.09375
- query_bias: float32 [1024], P('tp'), may hold values from -4 to 4
- value_bias: float32 [1024], P('tp'), may hold values from -0.75 to 0.75
- memory_qbias: float32 [1024], P('tp'), may hold values from -4 to 4
- memory_vbias: float32 [1024], P('tp'), may hold values from -0.75 to 0.75
- up_bias: float32 [4096], P('tp'), may hold values from -4 to 4
- out_bias: float32 [1024], replicated, may hold values from -4 to 4
- memory_obias: float32 [1024], replicated, may hold values from -4 to 4
- down_bias: float32 [1024], replicated, may hold values from -4 to 4
- gain_self: float32 [1024], replicated, may hold values from 0.5 to 1.5
- shift_self: float32 [1024], replicated, may hold values from -4 to 4
- gain_memory: float32 [1024], replicated, may hold values from 0.5 to 1.5
- shift_memory: float32 [1024], replicated, may hold values from -4 to 4
- gain_dense: float32 [1024], replicated, may hold values from 0.5 to 1.5
- shift_dense: float32 [1024], replicated, may hold values from -4 to 4
Outputs:
- outputs: bfloat16 [4, 2048, 1024], P('shard', ('ctx', 'tp'))
- inputs_grad: float32 [4, 2048, 1024], P('shard', ('ctx', 'tp'))
- encoded_grad: float32 [4, 512, 1024], P('shard', ('ctx', 'tp'))
- query_weight_grad: float32 [1024, 1024], P(('shard', 'ctx'), 'tp')
- key_weight_grad: float32 [1024, 1024], P(('shard', 'ctx'), 'tp')
- value_weight_grad: float32 [1024, 1024], P(('shard', 'ctx'), 'tp')
- out_weight_grad: float32 [1024, 1024], P('tp', ('shard', 'ctx'))
- memory_query_grad: float32 [1024, 1024], P(('shard', 'ctx'), 'tp')
- memory_key_grad: float32 [1024, 1024], P(('shard', 'ctx'), 'tp')
- memory_value_grad: float32 [1024, 1024], P(('shard', 'ctx'), 'tp')
- memory_out_grad: float32 [1024, 1024], P('tp', ('shard', 'ctx'))
- up_weight_grad: float32 [1024, 4096], P(('shard', 'ctx'), 'tp')
- down_weight_grad: float32 [4096, 1024], P('tp', ('shard', 'ctx'))
- query_bias_grad: float32 [1024], P('tp')
- value_bias_grad: float32 [1024], P('tp')
- memory_qbias_grad: float32 [1024], P('tp')
- memory_vbias_grad: float32 [1024], P('tp')
- up_bias_grad: float32 [4096], P('tp')
- out_bias_grad: float32 [1024], replicated
- memory_obias_grad: float32 [1024], replicated
- down_bias_grad: float32 [1024], replicated
- gain_self_grad: float32 [1024], replicated
- shift_self_grad: float32 [1024], replicated
- gain_memory_grad: float32 [1024], replicated
- shift_memory_grad: float32 [1024], replicated
- gain_dense_grad: float32 [1024], replicated
- shift_dense_grad: float32 [1024], replicated
The draws below stay inside these ranges and needn't reach their ends.
Inputs may be any that keep to these rules, and one draw needn't show every extreme that they name: `doc_lengths`: each row holds the 4 document lengths of one packed sequence in order; they sum to 2048, and the longest is exactly 1025.
All inputs are finite; a program needn't handle non-finite values.
Results may differ from the reference program's by a relative error of at most 0.025.
Values may be sent and summed in bfloat16 or wider, within the bound.
No kernel may reach another device: no remote copies, remote signals or barrier semaphores. Data moves between devices by JAX's collectives and lax.ppermute only.
A program may use at most 192 MiB of HBM per device.

```python
import math
import jax
import jax.numpy as jnp
import numpy as np
from jax import lax

D = 1024
HEADS = 16
FF = 4096
HDIM = 64
W = 1024
NDOC = 4
TOK_DEV = 1024
NSEQ = 4
LEN = 2048
ENC = 512


def level_of(stream_key, shape, cuts, least, high):
    def one(dim, parts):
        steps = jax.random.uniform(jax.random.fold_in(jax.random.fold_in(stream_key, 6), dim), (parts,), jnp.float32, least / len(cuts), high / len(cuts))
        return jnp.repeat(jnp.exp(steps), shape[dim] // parts).reshape((-1,) + (1,) * (len(shape) - dim - 1))

    level = one(*cuts[0])
    for cut in cuts[1:]:
        level = level * one(*cut)
    return level


def split_up(number_of, total, reach, skew):
    loads = [(1 << 20) // math.isqrt(rank ** skew) + 1 for rank in range(2, number_of + 1)]
    rest, holding = total - reach - (number_of - 1), [1] * (number_of - 1)
    while rest > 0:
        candidates = [i for i in range(number_of - 1) if holding[i] < reach]
        pool, left = sum([loads[i] for i in candidates]), rest
        for i in candidates:
            extra = min(reach - holding[i], max(1, left * loads[i] // pool), rest)
            holding[i] = holding[i] + extra
            rest = rest - extra
    return np.array([reach] + holding)


def uneven_parts(key, count, total, bound, skew):
    if count == 2:
        one = jax.random.randint(key, (), max(1, total - bound), min(bound, total - 1) + 1)
        return jnp.stack([one, total - one])
    lengths = jnp.asarray(split_up(count, total, bound, skew), jnp.int32)
    pairs = (count - 1) // 2
    source_of, taker = lengths[1:1 + 2 * pairs:2], lengths[2:2 + 2 * pairs:2]
    slack = jnp.minimum(source_of - 1, bound - taker)
    moved = jax.random.randint(jax.random.fold_in(key, 1), (pairs,), 0, 1 << 20) % (slack + 1)
    lengths = lengths.at[1:1 + 2 * pairs:2].set(source_of - moved).at[2:2 + 2 * pairs:2].set(taker + moved)
    return lengths[jax.random.permutation(jax.random.fold_in(key, 2), count)]


def normal_values(stream_key, dims, width, most, split=(), kind=jnp.bfloat16):
    loudness = level_of(stream_key, dims, split, -0.22, 0.18) if split else 1.0
    drawn = jax.random.normal(stream_key, dims, jnp.float32) * width * loudness
    return jnp.minimum(jnp.maximum(drawn, -most), most).astype(kind)


def setup_inputs(seed: int = 0) -> dict:
    key_of = jax.random.split(jax.random.key(seed), 29)
    inputs = normal_values(key_of[0], (NSEQ, LEN, D), 1.0, 6.0, ((0, 4), (1, 8)))
    encoded = normal_values(key_of[1], (NSEQ, ENC, D), 1.0, 6.0, ((0, 4), (1, 2)))
    doc_lengths = jax.vmap(lambda own: uneven_parts(own, NDOC, LEN, LEN - TOK_DEV + 1, 2))(jax.random.split(key_of[2], NSEQ)).reshape((NSEQ, NDOC)).astype(jnp.int32)
    cotangent = normal_values(key_of[3], (NSEQ, LEN, D), 1.0, 6.0, ((0, 4), (1, 8)))
    query_weight = normal_values(key_of[4], (D, D), D ** -0.5, 0.1875, ((0, 4), (1, 4)))
    key_weight = normal_values(key_of[5], (D, D), D ** -0.5, 0.1875, ((0, 4), (1, 4)))
    value_weight = normal_values(key_of[6], (D, D), D ** -0.5, 0.1875, ((0, 4), (1, 4)))
    out_weight = normal_values(key_of[7], (D, D), (max(1, D // 256)) ** -0.5, 3.0, ((0, 4), (1, 4)))
    memory_query = normal_values(key_of[8], (D, D), D ** -0.5, 0.1875, ((0, 4), (1, 4)))
    memory_key = normal_values(key_of[9], (D, D), D ** -0.5, 0.1875, ((0, 4), (1, 4)))
    memory_value = normal_values(key_of[10], (D, D), D ** -0.5, 0.1875, ((0, 4), (1, 4)))
    memory_out = normal_values(key_of[11], (D, D), (max(1, D // 512)) ** -0.5, 4.0, ((0, 4), (1, 4)))
    up_weight = normal_values(key_of[12], (D, FF), D ** -0.5, 0.1875, ((0, 4), (1, 4)))
    down_weight = normal_values(key_of[13], (FF, D), FF ** -0.5, 0.09375, ((0, 4), (1, 4)))
    query_bias = normal_values(key_of[14], (D,), 0.3, 4.0, ((0, 4),), jnp.float32)
    value_bias = normal_values(key_of[15], (D,), 0.05, 0.75, ((0, 4),), jnp.float32)
    memory_qbias = normal_values(key_of[16], (D,), 0.3, 4.0, ((0, 4),), jnp.float32)
    memory_vbias = normal_values(key_of[17], (D,), 0.05, 0.75, ((0, 4),), jnp.float32)
    up_bias = normal_values(key_of[18], (FF,), 0.3, 4.0, ((0, 4),), jnp.float32)
    out_bias = normal_values(key_of[19], (D,), 0.3, 4.0, (), jnp.float32)
    memory_obias = normal_values(key_of[20], (D,), 0.3, 4.0, (), jnp.float32)
    down_bias = normal_values(key_of[21], (D,), 0.3, 4.0, (), jnp.float32)
    gain_self = jnp.clip(1.0 + 0.1 * jax.random.normal(key_of[22], (D,), jnp.float32), 0.5, 1.5)
    shift_self = normal_values(key_of[23], (D,), 0.3, 4.0, (), jnp.float32)
    gain_memory = jnp.clip(1.0 + 0.1 * jax.random.normal(key_of[24], (D,), jnp.float32), 0.5, 1.5)
    shift_memory = normal_values(key_of[25], (D,), 0.3, 4.0, (), jnp.float32)
    gain_dense = jnp.clip(1.0 + 0.1 * jax.random.normal(key_of[26], (D,), jnp.float32), 0.5, 1.5)
    shift_dense = normal_values(key_of[27], (D,), 0.3, 4.0, (), jnp.float32)
    return dict(inputs=inputs, encoded=encoded, doc_lengths=doc_lengths, cotangent=cotangent, query_weight=query_weight, key_weight=key_weight, value_weight=value_weight, out_weight=out_weight, memory_query=memory_query, memory_key=memory_key, memory_value=memory_value, memory_out=memory_out, up_weight=up_weight, down_weight=down_weight, query_bias=query_bias, value_bias=value_bias, memory_qbias=memory_qbias, memory_vbias=memory_vbias, up_bias=up_bias, out_bias=out_bias, memory_obias=memory_obias, down_bias=down_bias, gain_self=gain_self, shift_self=shift_self, gain_memory=gain_memory, shift_memory=shift_memory, gain_dense=gain_dense, shift_dense=shift_dense)


HIGHEST = lax.Precision.HIGHEST
EPSILON = 1e-05
NEGATIVE = -1e+30

@jax.custom_vjp
def low(v):
    return lax.optimization_barrier(v.astype(jnp.bfloat16)).astype(jnp.float32)

@jax.custom_vjp
def low_back(v):
    return v

def low_keep(v):
    return (low(v), None)

def low_pass(kept, grad):
    return (grad,)

def back_keep(v):
    return (v, None)

def back_low(kept, grad):
    return (low(grad),)
low.defvjp(low_keep, low_pass)
low_back.defvjp(back_keep, back_low)

def narrow(value):
    return low(low_back(value))

def matmul(left, right):
    return jnp.dot(left, right, precision=HIGHEST)

def layer_norm(value, gain, shift):
    centre = value - lax.optimization_barrier(jnp.mean(value, axis=-1, keepdims=True))
    rstd = lax.rsqrt(lax.optimization_barrier(jnp.mean(centre * centre, axis=-1, keepdims=True)) + EPSILON)
    return centre * rstd * gain + shift

def probabilities(query, keys, allowed):
    scores = low_back(jnp.einsum('qhd,khd->hqk', query, keys, precision=HIGHEST))
    scores = jnp.where(allowed, scores, NEGATIVE)
    top = lax.optimization_barrier(jnp.max(scores, axis=-1, keepdims=True))
    expo = jnp.where(allowed, jnp.exp(scores - top), 0.0)
    return expo / lax.optimization_barrier(jnp.sum(expo, axis=-1, keepdims=True))

def mixing(probs, values):
    return jnp.einsum('hqk,khd->qhd', low(probs), values, precision=HIGHEST)

def self_attention(query, keys, values, segment):
    block = min(512, TOK_DEV)
    zeros = jnp.zeros((W,) + keys.shape[1:], jnp.float32)
    keys_pad = jnp.concatenate([zeros, keys], axis=0)
    values_pad = jnp.concatenate([zeros, values], axis=0)
    segment_pad = jnp.concatenate([jnp.zeros((W,), jnp.int32) - 1, segment], axis=0)

    @jax.checkpoint
    def one_block(index):
        start = index * block
        pos_query = start + jnp.arange(block, dtype=jnp.int32)
        pos_key = start - W + jnp.arange(block + W, dtype=jnp.int32)
        seg_query = lax.dynamic_slice_in_dim(segment, start, block, 0)
        seg_key = lax.dynamic_slice_in_dim(segment_pad, start, block + W, 0)
        allowed = (seg_query[:, None] == seg_key[None, :]) & (pos_key[None, :] <= pos_query[:, None])
        allowed = allowed & (pos_key[None, :] > pos_query[:, None] - W) & (pos_key[None, :] >= 0)
        probs = probabilities(lax.dynamic_slice_in_dim(query, start, block, 0), lax.dynamic_slice_in_dim(keys_pad, start, block + W, 0), allowed[None])
        return mixing(probs, lax.dynamic_slice_in_dim(values_pad, start, block + W, 0))
    mixed = lax.map(one_block, jnp.arange(LEN // block, dtype=jnp.int32))
    return mixed.reshape(LEN, HEADS * HDIM)

def cross_attention(query, keys, values):
    block = min(512, TOK_DEV)

    @jax.checkpoint
    def one_block(index):
        part = lax.dynamic_slice_in_dim(query, index * block, block, 0)
        return mixing(probabilities(part, keys, True), values)
    mixed = lax.map(one_block, jnp.arange(LEN // block, dtype=jnp.int32))
    return mixed.reshape(LEN, HEADS * HDIM)

def one_sequence(params, inputs_seq, encoded_seq, lengths_seq):
    query_weight, key_weight, value_weight, out_weight, memory_query, memory_key, memory_value, memory_out, up_weight, down_weight, query_bias, value_bias, memory_qbias, memory_vbias, up_bias, out_bias, memory_obias, down_bias, gain_self, shift_self, gain_memory, shift_memory, gain_dense, shift_dense = params
    ends = jnp.cumsum(lengths_seq, dtype=jnp.int32)
    positions = jnp.arange(LEN, dtype=jnp.int32)
    segment = lax.optimization_barrier(jnp.sum((positions[:, None] >= ends[None, :]).astype(jnp.int32), axis=1))
    query = narrow((matmul(inputs_seq, query_weight) + query_bias) * 0.125).reshape(LEN, HEADS, HDIM)
    keys = narrow(matmul(inputs_seq, key_weight)).reshape(LEN, HEADS, HDIM)
    values = narrow(matmul(inputs_seq, value_weight) + value_bias).reshape(LEN, HEADS, HDIM)
    self_mixed = narrow(self_attention(query, keys, values, segment))
    attended = low_back(matmul(self_mixed, out_weight) + out_bias)
    first = layer_norm(inputs_seq + attended, gain_self, shift_self)
    mquery = narrow((matmul(low(first), memory_query) + memory_qbias) * 0.125).reshape(LEN, HEADS, HDIM)
    mkeys = narrow(matmul(encoded_seq, memory_key)).reshape(ENC, HEADS, HDIM)
    mvalues = narrow(matmul(encoded_seq, memory_value) + memory_vbias).reshape(ENC, HEADS, HDIM)
    cross_mixed = narrow(cross_attention(mquery, mkeys, mvalues))
    crossed = low_back(matmul(cross_mixed, memory_out) + memory_obias)
    second = layer_norm(first + crossed, gain_memory, shift_memory)
    hidden = low_back(matmul(low(second), up_weight) + up_bias)
    act = low(jax.nn.gelu(hidden, approximate=False))
    dense = low_back(matmul(act, down_weight) + down_bias)
    return layer_norm(second + dense, gain_dense, shift_dense)

def reference(inputs, encoded, doc_lengths, cotangent, query_weight, key_weight, value_weight, out_weight, memory_query, memory_key, memory_value, memory_out, up_weight, down_weight, query_bias, value_bias, memory_qbias, memory_vbias, up_bias, out_bias, memory_obias, down_bias, gain_self, shift_self, gain_memory, shift_memory, gain_dense, shift_dense):
    params = tuple((item.astype(jnp.float32) for item in (query_weight, key_weight, value_weight, out_weight, memory_query, memory_key, memory_value, memory_out, up_weight, down_weight, query_bias, value_bias, memory_qbias, memory_vbias, up_bias, out_bias, memory_obias, down_bias, gain_self, shift_self, gain_memory, shift_memory, gain_dense, shift_dense)))

    def forward(inputs_all, encoded_all, params_all):
        step = jax.checkpoint(lambda item: one_sequence(params_all, item[0], item[1], item[2]))
        return lax.map(step, (inputs_all, encoded_all, doc_lengths))
    result, pullback = jax.vjp(forward, inputs.astype(jnp.float32), encoded.astype(jnp.float32), params)
    inputs_grad, encoded_grad, grads = pullback(cotangent.astype(jnp.float32))
    return (result.astype(jnp.bfloat16), inputs_grad, encoded_grad, grads[0], grads[1], grads[2], grads[3], grads[4], grads[5], grads[6], grads[7], grads[8], grads[9], grads[10], grads[11], grads[12], grads[13], grads[14], grads[15], grads[16], grads[17], grads[18], grads[19], grads[20], grads[21], grads[22], grads[23])
```

```python
from functools import partial

import jax
import jax.numpy as jnp
from jax import lax
from jax.experimental import pallas as pl
from jax.experimental.pallas import tpu as pltpu
from jax.sharding import PartitionSpec as P

HDIM = 64
W = 1024
TILE = 256
CHAINS = 1


EPSILON = 1e-05
NEGATIVE = -1e30
VMEM = 56 * 1024 * 1024


def matmul(left, right):
    return jnp.dot(left, right, preferred_element_type=jnp.float32)


def contract(form, left, right):
    return jnp.einsum(form, left, right, preferred_element_type=jnp.float32)


def low(value):
    return value.astype(jnp.bfloat16)


def wide(value):
    return value.astype(jnp.float32)


def swap(array, axis, bit):
    return lax.ppermute(array, axis, [(i, i ^ bit) for i in range(lax.axis_size(axis))])


def shift(array, axis, by):
    count = lax.axis_size(axis)
    pairs = [(i, i + by) for i in range(count) if 0 <= i + by < count]
    return lax.ppermute(array, axis, pairs)


def gather_direct(piece, axis):
    return [piece] + [swap(piece, axis, m) for m in range(1, lax.axis_size(axis))]


def gather_tree(piece, axis):
    count = lax.axis_size(axis)
    pieces = {0: piece}
    bit = count // 2
    while bit:
        for m in sorted(pieces):
            pieces[m | bit] = swap(pieces[m], axis, bit)
        bit //= 2
    return [pieces[m] for m in range(count)]


def scatter_tree(terms, axis):
    terms = list(terms)
    bit = 1
    while bit < len(terms):
        for m in reversed(range(bit, len(terms), 2 * bit)):
            arrived = swap(low(terms[m]), axis, bit)
            terms[m ^ bit] = wide(terms[m ^ bit]) + wide(arrived)
        bit *= 2
    return terms[0]


def scatter_direct(terms, axis):
    total = wide(terms[0])
    for m in range(1, lax.axis_size(axis)):
        total = total + wide(swap(low(terms[m]), axis, m))
    return total


def all_sum(value, axes):
    for axis in axes:
        bit = 1
        while bit < lax.axis_size(axis):
            value = value + swap(value, axis, bit)
            bit *= 2
    return value


def relative(array, dim, axis):
    count = lax.axis_size(axis)
    index = lax.axis_index(axis)
    size = array.shape[dim] // count
    blocks = [lax.slice_in_dim(array, m * size, (m + 1) * size, axis=dim) for m in range(count)]
    bit = 1
    while bit < count:
        odd = (index & bit) != 0
        blocks = [jnp.where(odd, blocks[m ^ bit], blocks[m]) for m in range(count)]
        bit *= 2
    return jnp.concatenate(blocks, axis=dim)


def stack_heads(value, heads):
    lane = lax.broadcasted_iota(jnp.int32, value.shape, 1) // HDIM
    zero = jnp.zeros_like(value)
    return jnp.concatenate([jnp.where(lane == h, value, zero) for h in range(heads)], axis=0)


def scores_of(rows, stacked, head, count):
    part = stacked[head * count : (head + 1) * count, :]
    return lax.dot_general(rows, part, (((1,), (1,)), ((), ())), preferred_element_type=jnp.float32)


def allowed_in(lower, key_start, query_start, shape):
    key = key_start + lax.broadcasted_iota(jnp.int32, shape, 0)
    query = query_start + lax.broadcasted_iota(jnp.int32, (1, shape[1]), 1)
    return (key >= lower) & (key <= query)


def attend_kernel(heads, masked, meta, *refs):
    if masked:
        lower_ref, query_ref, keys_ref, values_ref, old_keys_ref, old_values_ref = refs[:6]
        mixed_ref, mixed_t_ref, lse_ref, acc_ref = refs[6:]
        lower = lower_ref[...]
    else:
        query_ref, keys_ref, values_ref, mixed_ref, mixed_t_ref, lse_ref, acc_ref = refs
    step = pl.program_id(0)
    count = query_ref.shape[0]
    stacked = stack_heads(query_ref[...], heads)
    acc_ref[...] = jnp.zeros_like(acc_ref)
    tile = lax.bitwise_xor(step, meta[0])

    def add(carry, keys_from, values_from, place, key_tile, masking):
        rows = pl.ds(pl.multiple_of(place * count, count), count)
        keys, values_t = keys_from[rows, :], values_from[rows, :].T
        out = []
        for h in range(heads):
            top, total = carry[h]
            scores = scores_of(keys, stacked, h, count)
            if masking:
                ok = allowed_in(lower, key_tile * count, tile * count, scores.shape)
                scores = jnp.where(ok, scores, NEGATIVE)
            higher = jnp.maximum(top, jnp.max(scores, axis=0, keepdims=True))
            expo = jnp.exp(scores - higher)
            scale = jnp.exp(top - higher)
            part = slice(h * HDIM, (h + 1) * HDIM)
            acc_ref[part, :] = acc_ref[part, :] * scale + matmul(values_t[part, :], low(expo))
            out.append((higher, total * scale + jnp.sum(expo, axis=0, keepdims=True)))
        return tuple(out)

    first = jnp.full((1, count), NEGATIVE, jnp.float32)
    carry = tuple((first, jnp.zeros((1, count), jnp.float32)) for _ in range(heads))
    if masked:
        least = meta[1 + step]
        here = lambda n, c: add(
            c, keys_ref, values_ref, lax.bitwise_xor(tile - n, meta[0]), tile - n, True
        )
        carry = lax.fori_loop(0, tile - jnp.maximum(least, 0) + 1, here, carry)
        tiles = old_keys_ref.shape[0] // count
        before = lambda n, c: add(
            c, old_keys_ref, old_values_ref, lax.bitwise_xor(n + tiles, meta[0]), n, True
        )
        carry = lax.fori_loop(least, 0, before, carry)
    else:
        every = lambda n, c: add(c, keys_ref, values_ref, n, n, False)
        carry = lax.fori_loop(0, keys_ref.shape[0] // count, every, carry)
    for h in range(heads):
        top, total = carry[h]
        part = slice(h * HDIM, (h + 1) * HDIM)
        mixed_t_ref[part, :] = acc_ref[part, :] / total
        lse_ref[h : h + 1, :] = top + jnp.log(total)
    mixed_ref[...] = low(mixed_t_ref[...].T)


def attend_back_kernel(heads, masked, old, meta, *refs):
    refs = list(refs)
    lower = refs.pop(0)[...] if masked else None
    start_ref = refs.pop(0) if masked and not old else None
    query_ref, grad_ref, mixed_t_ref, lse_ref, keys_ref, values_ref = refs[:6]
    grad_query_ref, grad_keys_ref, grad_values_ref, keys_acc, values_acc, query_acc = refs[6:]
    step = pl.program_id(0)
    count = query_ref.shape[0]

    @pl.when(step == 0)
    def _():
        keys_acc[...] = jnp.zeros_like(keys_acc)
        values_acc[...] = jnp.zeros_like(values_acc)

    tile = lax.bitwise_xor(step, meta[0])
    if start_ref is None:
        query_acc[...] = jnp.zeros_like(query_acc)
    else:
        query_acc[...] = start_ref[...]
    stacked = stack_heads(query_ref[...], heads)
    grad = grad_ref[...]
    stacked_grad = stack_heads(grad, heads)
    weighed = wide(grad.T) * mixed_t_ref[...]
    lse = lse_ref[...]
    inner = [
        jnp.sum(weighed[h * HDIM : (h + 1) * HDIM, :], axis=0, keepdims=True) for h in range(heads)
    ]

    def add(place, key_tile):
        rows = pl.ds(pl.multiple_of(place * count, count), count)
        keys, values = keys_ref[rows, :], values_ref[rows, :]
        keys_t = keys.T
        probs, slopes = [], []
        if masked:
            ok = allowed_in(lower, key_tile * count, tile * count, (count, count))
        for h in range(heads):
            expo = jnp.exp(scores_of(keys, stacked, h, count) - lse[h : h + 1, :])
            if masked:
                expo = jnp.where(ok, expo, 0.0)
            slope = low(expo * (scores_of(values, stacked_grad, h, count) - inner[h]))
            part = slice(h * HDIM, (h + 1) * HDIM)
            query_acc[part, :] += matmul(keys_t[part, :], slope)
            probs.append(low(expo))
            slopes.append(slope)
        values_acc[rows, :] += matmul(jnp.concatenate(probs, axis=1), stacked_grad)
        keys_acc[rows, :] += matmul(jnp.concatenate(slopes, axis=1), stacked)

    if not masked:
        pl.loop(0, keys_ref.shape[0] // count)(lambda n: add(n, n))
    elif old:
        tiles = keys_ref.shape[0] // count
        pl.loop(meta[1 + step], 0)(lambda n: add(lax.bitwise_xor(n + tiles, meta[0]), n))
    else:
        pl.loop(jnp.maximum(meta[1 + step], 0), tile + 1)(
            lambda n: add(lax.bitwise_xor(n, meta[0]), n)
        )
    if old:
        grad_query_ref[...] = query_acc[...]
    else:
        grad_query_ref[...] = low(query_acc[...].T)

    @pl.when(step == pl.num_programs(0) - 1)
    def _():
        grad_keys_ref[...] = keys_acc[...].astype(grad_keys_ref.dtype)
        grad_values_ref[...] = values_acc[...].astype(grad_values_ref.dtype)


def tiled(width, column):
    return pl.BlockSpec((TILE, width), lambda t, meta: (t, column))


def tiled_t(height):
    return pl.BlockSpec((height, TILE), lambda t, meta: (0, t))


def entire(rows, width, column):
    return pl.BlockSpec((rows, width), lambda t, meta: (0, column))


def attend(meta, lower, query, keys, values, width, before=None):
    rows = query[0].shape[0]
    count = keys[0].shape[0]
    heads = width // HDIM
    masked = before is not None
    inputs = [query[0], keys[0], values[0]]
    specs = [
        tiled(width, query[1]),
        entire(count, width, keys[1]),
        entire(count, width, values[1]),
    ]
    if masked:
        inputs = [lower] + inputs + [before[0], before[0]]
        specs = [tiled_t(1)] + specs
        specs += [entire(before[0].shape[0], width, 0), entire(before[0].shape[0], width, 1)]
    pairs = rows * count * width
    return pl.pallas_call(
        partial(attend_kernel, heads, masked),
        grid_spec=pltpu.PrefetchScalarGridSpec(
            num_scalar_prefetch=1,
            grid=(rows // TILE,),
            in_specs=specs,
            out_specs=[tiled(width, 0), tiled_t(width), tiled_t(heads)],
            scratch_shapes=[pltpu.VMEM((width, TILE), jnp.float32)],
        ),
        out_shape=[
            jax.ShapeDtypeStruct((rows, width), jnp.bfloat16),
            jax.ShapeDtypeStruct((width, rows), jnp.float32),
            jax.ShapeDtypeStruct((heads, rows), jnp.float32),
        ],
        compiler_params=pltpu.CompilerParams(vmem_limit_bytes=VMEM),
        cost_estimate=pl.CostEstimate(
            flops=8 * pairs, bytes_accessed=2 * (rows + count) * width * 2, transcendentals=0
        ),
    )(meta, *inputs)


def attend_back(meta, lower, query, grad, mixed_t, lse, keys, values, width, kind, start=None):
    rows = query[0].shape[0]
    count = keys[0].shape[0]
    heads = width // HDIM
    masked = kind != "cross"
    old = kind == "old"
    inputs = [query[0], grad, mixed_t, lse, keys[0], values[0]]
    specs = [
        tiled(width, query[1]),
        tiled(width, 0),
        tiled_t(width),
        tiled_t(heads),
        entire(count, width, keys[1]),
        entire(count, width, values[1]),
    ]
    if start is not None:
        inputs, specs = [start] + inputs, [tiled_t(width)] + specs
    if masked:
        inputs, specs = [lower] + inputs, [tiled_t(1)] + specs
    kept = jnp.bfloat16 if masked else jnp.float32
    pairs = rows * count * width
    return pl.pallas_call(
        partial(attend_back_kernel, heads, masked, old),
        grid_spec=pltpu.PrefetchScalarGridSpec(
            num_scalar_prefetch=1,
            grid=(rows // TILE,),
            in_specs=specs,
            out_specs=[
                tiled_t(width) if old else tiled(width, 0),
                entire(count, width, 0),
                entire(count, width, 0),
            ],
            scratch_shapes=[
                pltpu.VMEM((count, width), jnp.float32),
                pltpu.VMEM((count, width), jnp.float32),
                pltpu.VMEM((width, TILE), jnp.float32),
            ],
        ),
        out_shape=[
            jax.ShapeDtypeStruct((width, rows), jnp.float32)
            if old
            else jax.ShapeDtypeStruct((rows, width), jnp.bfloat16),
            jax.ShapeDtypeStruct((count, width), kept),
            jax.ShapeDtypeStruct((count, width), kept),
        ],
        compiler_params=pltpu.CompilerParams(vmem_limit_bytes=VMEM),
        cost_estimate=pl.CostEstimate(
            flops=20 * pairs, bytes_accessed=4 * (rows + count) * width * 2, transcendentals=0
        ),
    )(meta, *inputs)


def layer_norm(value, gain, shift_by):
    centre = value - jnp.mean(value, axis=-1, keepdims=True)
    rstd = lax.rsqrt(jnp.mean(centre * centre, axis=-1, keepdims=True) + EPSILON)
    normed = centre * rstd
    return (normed * gain + shift_by, normed, rstd)


def norm_back(grad_out, normed, rstd, gain):
    scaled = grad_out * gain
    inner = scaled - jnp.mean(scaled, axis=-1, keepdims=True)
    inner = inner - normed * jnp.mean(scaled * normed, axis=-1, keepdims=True)
    return (rstd * inner, jnp.sum(grad_out * normed, axis=0), jnp.sum(grad_out, axis=0))


def gelu_and_slope(value):
    phi = 0.5 * (1.0 + lax.erf(value * 0.7071067811865476))
    bell = jnp.exp(-0.5 * value * value) * 0.3989422804014327
    return value * phi, phi + value * bell


def column_sum(value):
    return jnp.sum(wide(value), axis=0)


def scatter_rows(make, rows):
    count = lax.axis_size("tp")
    half = rows // 2
    far = low(make(slice(half, rows))).reshape(count // 2, rows // count, -1)
    near = low(make(slice(0, half))).reshape(count // 2, rows // count, -1)
    terms = [near[m] for m in range(count // 2)] + [far[m] for m in range(count // 2)]
    return scatter_tree(terms, "tp")


def gather_rows(piece):
    return jnp.concatenate(gather_tree(piece, "tp"), axis=0)


def scatter_weight(grad):
    shards, ctxs = lax.axis_size("shard"), lax.axis_size("ctx")
    blocks = low(grad).reshape(shards, ctxs, -1, grad.shape[1])
    mine = lax.axis_index("ctx")
    terms = [
        lax.dynamic_index_in_dim(blocks, mine ^ m, axis=1, keepdims=False) for m in range(ctxs)
    ]
    total = scatter_direct(terms, "ctx")
    return scatter_direct([total[m] for m in range(shards)], "shard")


def scatter_weight_t(grad):
    shards, ctxs = lax.axis_size("shard"), lax.axis_size("ctx")
    rows, columns = grad.shape
    size = columns // (shards * ctxs)
    mine = lax.axis_index("ctx")
    kept = low(grad)
    blocks = [kept[:, s * size : (s + 1) * size] for s in range(shards * ctxs)]
    bit = 1
    while bit < ctxs:
        odd = (mine & bit) != 0
        blocks = [jnp.where(odd, blocks[s ^ bit], blocks[s]) for s in range(shards * ctxs)]
        bit *= 2
    terms = [jnp.stack([blocks[s * ctxs + m] for s in range(shards)]) for m in range(ctxs)]
    total = scatter_direct(terms, "ctx")
    return scatter_direct([total[m] for m in range(shards)], "shard")


def per_device(
    inputs,
    encoded,
    doc_lengths,
    cotangent,
    query_weight,
    key_weight,
    value_weight,
    out_weight,
    memory_query,
    memory_key,
    memory_value,
    memory_out,
    up_weight,
    down_weight,
    query_bias,
    value_bias,
    memory_qbias,
    memory_vbias,
    up_bias,
    out_bias,
    memory_obias,
    down_bias,
    gain_self,
    shift_self,
    gain_memory,
    shift_memory,
    gain_dense,
    shift_dense,
):
    tps = lax.axis_size("tp")
    tp_index = lax.axis_index("tp")
    share_rows = inputs.shape[1]
    rows = share_rows * tps
    width = query_weight.shape[1]
    base = lax.axis_index("ctx") * rows

    def gather_in(weight):
        return jnp.concatenate(gather_direct(weight, "shard"), axis=0)

    def gather_out(weight):
        return jnp.concatenate(gather_direct(weight, "shard"), axis=1)

    share = relative(inputs[0], 1, "shard")
    old_share = relative(shift(inputs[0], "ctx", 1), 1, "shard")
    inputs_rows = gather_rows(share)
    old_rows = gather_rows(old_share)
    qkv_full = gather_in(jnp.concatenate([query_weight, key_weight, value_weight], axis=1))
    out_full = gather_out(out_weight)
    states = relative(relative(encoded[0], 1, "shard"), 0, "tp")
    mkv_full = gather_in(jnp.concatenate([memory_key, memory_value], axis=1))
    mquery_full = gather_in(memory_query)
    mout_full = gather_out(memory_out)
    up_full = gather_in(up_weight)
    down_full = gather_out(down_weight)
    vectors = relative(
        jnp.stack(
            [
                out_bias,
                memory_obias,
                down_bias,
                gain_self,
                shift_self,
                gain_memory,
                shift_memory,
                gain_dense,
                shift_dense,
            ]
        ),
        1,
        "shard",
    )
    (
        out_bias,
        memory_obias,
        down_bias,
        gain_self,
        shift_self,
        gain_memory,
        shift_memory,
        gain_dense,
        shift_dense,
    ) = [vectors[i] for i in range(9)]
    upstream = wide(relative(cotangent[0], 1, "shard"))

    ends = jnp.cumsum(doc_lengths[0], dtype=jnp.int32)
    local = jnp.arange(rows, dtype=jnp.int32)
    place = base + (local // share_rows ^ tp_index) * share_rows + local % share_rows
    opens = jnp.max(jnp.where(place[:, None] >= ends[None, :], ends[None, :], 0), axis=1)
    lower = jnp.maximum(opens, place - (W - 1)) - base
    least = lower.reshape(-1, TILE)[:, 0] // TILE
    meta = jnp.concatenate([tp_index[None].astype(jnp.int32), least])
    lower = lower[None, :]

    zeros = jnp.zeros_like(query_bias)
    qkv = low(
        (matmul(inputs_rows, qkv_full) + jnp.concatenate([query_bias, zeros, value_bias]))
        * jnp.concatenate([zeros + 0.125, zeros + 1.0, zeros + 1.0])
    )
    old_kv = low(
        matmul(old_rows, qkv_full[:, width:]) + jnp.concatenate([zeros, value_bias])
    )
    self_mixed, self_mixed_t, self_lse = attend(
        meta, lower, (qkv, 0), (qkv, 1), (qkv, 2), width, (old_kv, None)
    )

    mkv_own = low(matmul(states, mkv_full) + jnp.concatenate([zeros, memory_vbias]))
    mkv = jnp.concatenate(gather_direct(mkv_own, "ctx"), axis=0)

    still = jnp.zeros((1,), jnp.int32)
    step_rows = share_rows // CHAINS
    chains = range(CHAINS)

    def chain_rows(array, c):
        if CHAINS == 1:
            return array
        split = array.reshape(tps, CHAINS, step_rows, array.shape[1])
        return split[:, c].reshape(tps * step_rows, array.shape[1])

    def own(array, c):
        return array[c * step_rows : (c + 1) * step_rows]

    count = tps * step_rows
    kept = []
    for c in chains:
        mixed = chain_rows(self_mixed, c)
        attn_share = scatter_rows(lambda s: matmul(mixed[s], out_full), count)
        first, normed_one, rstd_one = layer_norm(
            wide(own(share, c)) + attn_share + out_bias, gain_self, shift_self
        )
        first_rows = gather_rows(low(first))
        mquery = low((matmul(first_rows, mquery_full) + memory_qbias) * 0.125)
        cross_mixed, cross_mixed_t, cross_lse = attend(
            still, None, (mquery, 0), (mkv, 0), (mkv, 1), width
        )
        cross_share = scatter_rows(lambda s: matmul(cross_mixed[s], mout_full), count)
        second, normed_two, rstd_two = layer_norm(
            first + cross_share + memory_obias, gain_memory, shift_memory
        )
        second_rows = gather_rows(low(second))
        act, slope = gelu_and_slope(matmul(second_rows, up_full) + up_bias)
        act_low, slope_low = low(act), low(slope)
        dense_share = scatter_rows(lambda s: matmul(act_low[s], down_full), count)
        result, normed_three, rstd_three = layer_norm(
            second + dense_share + down_bias, gain_dense, shift_dense
        )
        grad_three, gain_dense_grad, shift_dense_grad = norm_back(
            own(upstream, c), normed_three, rstd_three, gain_dense
        )
        dense_low = low(grad_three)
        dense_rows = gather_rows(dense_low)
        hidden_low = low(contract("rd,fd->rf", dense_rows, down_full) * wide(slope_low))
        second_share = scatter_rows(
            lambda s: contract("rf,df->rd", hidden_low[s], up_full), count
        )
        grad_two, gain_memory_grad, shift_memory_grad = norm_back(
            grad_three + second_share, normed_two, rstd_two, gain_memory
        )
        cross_low = low(grad_two)
        cross_rows = gather_rows(cross_low)
        grad_cross_mixed = low(contract("rd,kd->rk", cross_rows, mout_full))
        mquery_back, mkeys_back, mvalues_back = attend_back(
            still,
            None,
            (mquery, 0),
            grad_cross_mixed,
            cross_mixed_t,
            cross_lse,
            (mkv, 0),
            (mkv, 1),
            width,
            "cross",
        )
        mquery_pre = mquery_back * 0.125
        first_share = scatter_rows(
            lambda s: contract("rk,dk->rd", mquery_pre[s], mquery_full), count
        )
        grad_one, gain_self_grad, shift_self_grad = norm_back(
            grad_two + first_share, normed_one, rstd_one, gain_self
        )
        self_low = low(grad_one)
        self_rows = gather_rows(self_low)
        grad_self = low(contract("rd,kd->rk", self_rows, out_full))
        kept.append(
            dict(
                result=low(result),
                grad_one=grad_one,
                grad_self=grad_self,
                mkeys=mkeys_back,
                mvalues=mvalues_back,
                out=contract("rk,rd->kd", mixed, self_rows),
                mquery=contract("rd,rk->dk", first_rows, mquery_pre),
                mout=contract("rk,rd->kd", cross_mixed, cross_rows),
                up=contract("rd,rf->df", second_rows, hidden_low),
                down=contract("rf,rd->fd", act_low, dense_rows),
                mquery_bias=column_sum(mquery_pre),
                up_bias=column_sum(hidden_low),
                early=jnp.stack(
                    [
                        column_sum(cross_low),
                        column_sum(dense_low),
                        gain_memory_grad,
                        shift_memory_grad,
                        gain_dense_grad,
                        shift_dense_grad,
                    ]
                ),
                late=jnp.stack([column_sum(self_low), gain_self_grad, shift_self_grad]),
            )
        )

    def total(name):
        value = kept[0][name]
        for other in kept[1:]:
            value = value + other[name]
        return value

    def joined(name):
        if CHAINS == 1:
            return kept[0][name]
        return jnp.concatenate([k[name] for k in kept], axis=0)

    def rows_joined(name):
        if CHAINS == 1:
            return kept[0][name]
        return jnp.stack([k[name].reshape(tps, step_rows, -1) for k in kept], axis=1).reshape(
            rows, -1
        )

    down_weight_grad = scatter_weight_t(total("down"))
    up_weight_grad = scatter_weight(total("up"))
    memory_out_grad = scatter_weight_t(total("mout"))
    memory_query_grad = scatter_weight(total("mquery"))

    own_states = states.shape[0]
    mkv_back = jnp.concatenate([total("mkeys"), total("mvalues")], axis=1)
    mkv_low = low(
        scatter_direct(
            [
                mkv_back[m * own_states : (m + 1) * own_states]
                for m in range(lax.axis_size("ctx"))
            ],
            "ctx",
        )
    )
    mkv_grad = scatter_weight(contract("ed,ek->dk", states, mkv_low))
    memory_vbias_grad = column_sum(mkv_low[:, width:])
    encoded_grad = scatter_rows(
        lambda s: contract("ek,dk->ed", mkv_low[s], mkv_full), own_states
    )

    out_weight_grad = scatter_weight_t(total("out"))
    grad_self = rows_joined("grad_self")
    query_start, old_keys, old_values = attend_back(
        meta,
        lower,
        (qkv, 0),
        grad_self,
        self_mixed_t,
        self_lse,
        (old_kv, 0),
        (old_kv, 1),
        width,
        "old",
    )
    old_back = jnp.concatenate([old_keys, old_values], axis=1)
    back = shift(old_back, "ctx", -1)
    query_back, keys_back, values_back = attend_back(
        meta,
        lower,
        (qkv, 0),
        grad_self,
        self_mixed_t,
        self_lse,
        (qkv, 1),
        (qkv, 2),
        width,
        "own",
        query_start,
    )
    query_pre = query_back * 0.125
    kv_back = jnp.concatenate([keys_back, values_back], axis=1)
    kv_grad = contract("rd,rk->dk", inputs_rows, kv_back) + contract(
        "rd,rk->dk", old_rows, old_back
    )
    kv_weight_grad = scatter_weight(kv_grad)
    query_weight_grad = scatter_weight(contract("rd,rk->dk", inputs_rows, query_pre))
    value_bias_grad = column_sum(values_back) + column_sum(old_values)
    kv_all = low(wide(kv_back) + wide(back))

    def inputs_term(s):
        term = contract("rk,dk->rd", query_pre[s], qkv_full[:, :width])
        return term + contract("rk,dk->rd", kv_all[s], qkv_full[:, width:])

    inputs_grad = joined("grad_one") + scatter_rows(inputs_term, rows)

    early = relative(total("early"), 1, "shard")
    late = relative(total("late"), 1, "shard")
    early = all_sum(early, ("tp", "ctx", "shard"))
    late = all_sum(late, ("tp", "ctx", "shard"))
    early_split = all_sum(
        jnp.concatenate([total("mquery_bias"), memory_vbias_grad, total("up_bias")])[None],
        ("ctx", "shard"),
    )[0]
    late_split = all_sum(
        jnp.concatenate([column_sum(query_pre), value_bias_grad])[None], ("ctx", "shard")
    )[0]
    return (
        relative(joined("result"), 1, "shard")[None],
        relative(inputs_grad, 1, "shard")[None],
        relative(encoded_grad, 1, "shard")[None],
        query_weight_grad,
        kv_weight_grad[:, :width],
        kv_weight_grad[:, width:],
        out_weight_grad,
        memory_query_grad,
        mkv_grad[:, :width],
        mkv_grad[:, width:],
        memory_out_grad,
        up_weight_grad,
        down_weight_grad,
        late_split[:width],
        late_split[width:],
        early_split[:width],
        early_split[width : 2 * width],
        early_split[2 * width :],
        late[0],
        early[0],
        early[1],
        late[1],
        late[2],
        early[2],
        early[3],
        early[4],
        early[5],
    )


def solution(mesh):
    placed = (
        P("shard", ("ctx", "tp"), None),
        P("shard", "ctx", None),
        P("shard", None),
        P("shard", ("ctx", "tp"), None),
        P("shard", "tp"),
        P("shard", "tp"),
        P("shard", "tp"),
        P("tp", "shard"),
        P("shard", "tp"),
        P("shard", "tp"),
        P("shard", "tp"),
        P("tp", "shard"),
        P("shard", "tp"),
        P("tp", "shard"),
        P("tp"),
        P("tp"),
        P("tp"),
        P("tp"),
        P("tp"),
        P(),
        P(),
        P(),
        P(),
        P(),
        P(),
        P(),
        P(),
        P(),
    )
    return jax.shard_map(
        per_device,
        mesh=mesh,
        in_specs=placed,
        out_specs=(
            P("shard", ("ctx", "tp"), None),
            P("shard", ("ctx", "tp"), None),
            P("shard", ("ctx", "tp"), None),
            P(("shard", "ctx"), "tp"),
            P(("shard", "ctx"), "tp"),
            P(("shard", "ctx"), "tp"),
            P("tp", ("shard", "ctx")),
            P(("shard", "ctx"), "tp"),
            P(("shard", "ctx"), "tp"),
            P(("shard", "ctx"), "tp"),
            P("tp", ("shard", "ctx")),
            P(("shard", "ctx"), "tp"),
            P("tp", ("shard", "ctx")),
            P("tp"),
            P("tp"),
            P("tp"),
            P("tp"),
            P("tp"),
            P(),
            P(),
            P(),
            P(),
            P(),
            P(),
            P(),
            P(),
            P(),
        ),
        check_vma=False,
    )
```

```python
from functools import partial

import jax
import jax.numpy as jnp
from jax import lax
from jax.experimental import pallas as pl
from jax.experimental.pallas import tpu as pltpu
from jax.sharding import PartitionSpec as P

HDIM = 64
W = 1024
TILE = 256


EPSILON = 1e-05
NEGATIVE = -1e30
VMEM = 56 * 1024 * 1024


def matmul(left, right):
    return jnp.dot(left, right, preferred_element_type=jnp.float32)


def contract(form, left, right):
    return jnp.einsum(form, left, right, preferred_element_type=jnp.float32)


def low(value):
    return value.astype(jnp.bfloat16)


def wide(value):
    return value.astype(jnp.float32)


def swap(array, axis, bit):
    return lax.ppermute(array, axis, [(i, i ^ bit) for i in range(lax.axis_size(axis))])


def shift(array, axis, by):
    count = lax.axis_size(axis)
    pairs = [(i, i + by) for i in range(count) if 0 <= i + by < count]
    return lax.ppermute(array, axis, pairs)


def steps_of(*axes):
    steps = []
    for axis in axes:
        bit = lax.axis_size(axis) // 2
        while bit:
            steps.append((axis, bit))
            bit //= 2
    return steps


def after(value, *others):
    others = [other for other in others if other is not None]
    return lax.optimization_barrier((value, *others))[0] if others else value


def gather_tree(array, steps, start=None, used=None):
    for n, (axis, bit) in enumerate(steps):
        arrived = swap(after(array, start if n == 0 else None), axis, bit)
        array = jnp.concatenate([after(array, used if n == len(steps) - 1 else None), arrived])
    return array


def scatter_more(total, steps, start=None, used=None):
    for n, (axis, bit) in enumerate(reversed(steps)):
        half = total.shape[0] // 2
        arrived = swap(after(low(total[half:]), start if n == 0 else None), axis, bit)
        kept = after(total[:half], used if n == len(steps) - 1 else None)
        total = kept + wide(arrived)
    return total


def scatter_tree(make, size, steps, used=None):
    axis, bit = steps[-1]
    half = size // 2
    arrived = swap(low(make(slice(half, size))), axis, bit)
    total = after(make(slice(0, half)), used) + wide(arrived)
    return scatter_more(total, steps[:-1])


def all_sum(value, steps):
    for axis, bit in steps:
        value = value + swap(value, axis, bit)
    return value


def flat_bit(step, axes):
    axis, bit = step
    for other in axes[axes.index(axis) + 1 :]:
        bit = bit * lax.axis_size(other)
    return bit


def masks_of(axes, steps):
    masks = [0]
    for step in steps:
        masks = masks + [m | flat_bit(step, axes) for m in masks]
    return masks


def cross_over(blocks, axes):
    index = lax.axis_index(axes)
    bit = 1
    while bit < len(blocks):
        odd = (index & bit) != 0
        blocks = [jnp.where(odd, blocks[m ^ bit], blocks[m]) for m in range(len(blocks))]
        bit *= 2
    return blocks


def split(array, dim, count):
    size = array.shape[dim] // count
    return [lax.slice_in_dim(array, m * size, (m + 1) * size, axis=dim) for m in range(count)]


def to_tree(array, dim, axes, steps):
    masks = masks_of(axes, steps)
    blocks = cross_over(split(array, dim, len(masks)), axes)
    return jnp.concatenate([blocks[m] for m in masks], axis=dim)


def from_tree(array, dim, axes, steps):
    masks = masks_of(axes, steps)
    blocks = split(array, dim, len(masks))
    blocks = cross_over([blocks[masks.index(m)] for m in range(len(masks))], axes)
    return jnp.concatenate(blocks, axis=dim)


def in_tree(block, bits):
    return sum(((block >> k) & 1) << (bits - 1 - k) for k in range(bits))


def stack_heads(value, heads):
    lane = lax.broadcasted_iota(jnp.int32, value.shape, 1) // HDIM
    zero = jnp.zeros_like(value)
    return jnp.concatenate([jnp.where(lane == h, value, zero) for h in range(heads)], axis=0)


def scores_of(rows, stacked, head, count):
    part = stacked[head * count : (head + 1) * count, :]
    return lax.dot_general(rows, part, (((1,), (1,)), ((), ())), preferred_element_type=jnp.float32)


def allowed_in(lower, key_start, query_start, shape):
    key = key_start + lax.broadcasted_iota(jnp.int32, shape, 0)
    query = query_start + lax.broadcasted_iota(jnp.int32, (1, shape[1]), 1)
    return (key >= lower) & (key <= query)


def attend_kernel(heads, masked, bits, meta, *refs):
    if masked:
        lower_ref, query_ref, keys_ref, values_ref, old_keys_ref, old_values_ref = refs[:6]
        mixed_ref, mixed_t_ref, lse_ref, acc_ref = refs[6:]
        lower = lower_ref[...]
    else:
        query_ref, keys_ref, values_ref, mixed_ref, mixed_t_ref, lse_ref, acc_ref = refs
    step = pl.program_id(0)
    count = query_ref.shape[0]
    stacked = stack_heads(query_ref[...], heads)
    acc_ref[...] = jnp.zeros_like(acc_ref)
    tile = in_tree(step, bits) ^ meta[0]

    def add(carry, keys_from, values_from, place, key_tile, masking):
        rows = pl.ds(pl.multiple_of(place * count, count), count)
        keys, values_t = keys_from[rows, :], values_from[rows, :].T
        out = []
        for h in range(heads):
            top, total = carry[h]
            scores = scores_of(keys, stacked, h, count)
            if masking:
                ok = allowed_in(lower, key_tile * count, tile * count, scores.shape)
                scores = jnp.where(ok, scores, NEGATIVE)
            higher = jnp.maximum(top, jnp.max(scores, axis=0, keepdims=True))
            expo = jnp.exp(scores - higher)
            scale = jnp.exp(top - higher)
            part = slice(h * HDIM, (h + 1) * HDIM)
            acc_ref[part, :] = acc_ref[part, :] * scale + matmul(values_t[part, :], low(expo))
            out.append((higher, total * scale + jnp.sum(expo, axis=0, keepdims=True)))
        return tuple(out)

    first = jnp.full((1, count), NEGATIVE, jnp.float32)
    carry = tuple((first, jnp.zeros((1, count), jnp.float32)) for _ in range(heads))
    if masked:
        least = meta[1 + step]
        here = lambda n, c: add(
            c, keys_ref, values_ref, in_tree((tile - n) ^ meta[0], bits), tile - n, True
        )
        carry = lax.fori_loop(0, tile - jnp.maximum(least, 0) + 1, here, carry)
        tiles = old_keys_ref.shape[0] // count
        before = lambda n, c: add(
            c, old_keys_ref, old_values_ref, in_tree((n + tiles) ^ meta[0], bits), n, True
        )
        carry = lax.fori_loop(least, 0, before, carry)
    else:
        every = lambda n, c: add(c, keys_ref, values_ref, n, n, False)
        carry = lax.fori_loop(0, keys_ref.shape[0] // count, every, carry)
    for h in range(heads):
        top, total = carry[h]
        part = slice(h * HDIM, (h + 1) * HDIM)
        mixed_t_ref[part, :] = acc_ref[part, :] / total
        lse_ref[h : h + 1, :] = top + jnp.log(total)
    mixed_ref[...] = low(mixed_t_ref[...].T)


def attend_back_kernel(heads, masked, old, bits, meta, *refs):
    refs = list(refs)
    lower = refs.pop(0)[...] if masked else None
    start_ref = refs.pop(0) if masked and not old else None
    query_ref, grad_ref, mixed_t_ref, lse_ref, keys_ref, values_ref = refs[:6]
    grad_query_ref, grad_keys_ref, grad_values_ref, keys_acc, values_acc, query_acc = refs[6:]
    step = pl.program_id(0)
    count = query_ref.shape[0]

    @pl.when(step == 0)
    def _():
        keys_acc[...] = jnp.zeros_like(keys_acc)
        values_acc[...] = jnp.zeros_like(values_acc)

    tile = in_tree(step, bits) ^ meta[0]
    if start_ref is None:
        query_acc[...] = jnp.zeros_like(query_acc)
    else:
        query_acc[...] = start_ref[...]
    stacked = stack_heads(query_ref[...], heads)
    grad = grad_ref[...]
    stacked_grad = stack_heads(grad, heads)
    weighed = wide(grad.T) * mixed_t_ref[...]
    lse = lse_ref[...]
    inner = [
        jnp.sum(weighed[h * HDIM : (h + 1) * HDIM, :], axis=0, keepdims=True) for h in range(heads)
    ]

    def add(place, key_tile):
        rows = pl.ds(pl.multiple_of(place * count, count), count)
        keys, values = keys_ref[rows, :], values_ref[rows, :]
        keys_t = keys.T
        probs, slopes = [], []
        if masked:
            ok = allowed_in(lower, key_tile * count, tile * count, (count, count))
        for h in range(heads):
            expo = jnp.exp(scores_of(keys, stacked, h, count) - lse[h : h + 1, :])
            if masked:
                expo = jnp.where(ok, expo, 0.0)
            slope = low(expo * (scores_of(values, stacked_grad, h, count) - inner[h]))
            part = slice(h * HDIM, (h + 1) * HDIM)
            query_acc[part, :] += matmul(keys_t[part, :], slope)
            probs.append(low(expo))
            slopes.append(slope)
        values_acc[rows, :] += matmul(jnp.concatenate(probs, axis=1), stacked_grad)
        keys_acc[rows, :] += matmul(jnp.concatenate(slopes, axis=1), stacked)

    if not masked:
        pl.loop(0, keys_ref.shape[0] // count)(lambda n: add(n, n))
    elif old:
        tiles = keys_ref.shape[0] // count
        pl.loop(meta[1 + step], 0)(lambda n: add(in_tree((n + tiles) ^ meta[0], bits), n))
    else:
        pl.loop(jnp.maximum(meta[1 + step], 0), tile + 1)(
            lambda n: add(in_tree(n ^ meta[0], bits), n)
        )
    if old:
        grad_query_ref[...] = query_acc[...]
    else:
        grad_query_ref[...] = low(query_acc[...].T)

    @pl.when(step == pl.num_programs(0) - 1)
    def _():
        grad_keys_ref[...] = keys_acc[...].astype(grad_keys_ref.dtype)
        grad_values_ref[...] = values_acc[...].astype(grad_values_ref.dtype)


def tiled(width, column):
    return pl.BlockSpec((TILE, width), lambda t, meta: (t, column))


def tiled_t(height):
    return pl.BlockSpec((height, TILE), lambda t, meta: (0, t))


def entire(rows, width, column):
    return pl.BlockSpec((rows, width), lambda t, meta: (0, column))


def attend(meta, lower, query, keys, values, width, before=None):
    rows = query[0].shape[0]
    count = keys[0].shape[0]
    heads = width // HDIM
    masked = before is not None
    inputs = [query[0], keys[0], values[0]]
    specs = [
        tiled(width, query[1]),
        entire(count, width, keys[1]),
        entire(count, width, values[1]),
    ]
    if masked:
        inputs = [lower] + inputs + [before[0], before[0]]
        specs = [tiled_t(1)] + specs
        specs += [entire(before[0].shape[0], width, 0), entire(before[0].shape[0], width, 1)]
    pairs = rows * count * width
    return pl.pallas_call(
        partial(attend_kernel, heads, masked, (rows // TILE).bit_length() - 1),
        grid_spec=pltpu.PrefetchScalarGridSpec(
            num_scalar_prefetch=1,
            grid=(rows // TILE,),
            in_specs=specs,
            out_specs=[tiled(width, 0), tiled_t(width), tiled_t(heads)],
            scratch_shapes=[pltpu.VMEM((width, TILE), jnp.float32)],
        ),
        out_shape=[
            jax.ShapeDtypeStruct((rows, width), jnp.bfloat16),
            jax.ShapeDtypeStruct((width, rows), jnp.float32),
            jax.ShapeDtypeStruct((heads, rows), jnp.float32),
        ],
        compiler_params=pltpu.CompilerParams(vmem_limit_bytes=VMEM),
        cost_estimate=pl.CostEstimate(
            flops=64 * pairs, bytes_accessed=2 * (rows + count) * width * 2, transcendentals=0
        ),
    )(meta, *inputs)


def attend_back(meta, lower, query, grad, mixed_t, lse, keys, values, width, kind, start=None):
    rows = query[0].shape[0]
    count = keys[0].shape[0]
    heads = width // HDIM
    masked = kind != "cross"
    old = kind == "old"
    inputs = [query[0], grad, mixed_t, lse, keys[0], values[0]]
    specs = [
        tiled(width, query[1]),
        tiled(width, 0),
        tiled_t(width),
        tiled_t(heads),
        entire(count, width, keys[1]),
        entire(count, width, values[1]),
    ]
    if start is not None:
        inputs, specs = [start] + inputs, [tiled_t(width)] + specs
    if masked:
        inputs, specs = [lower] + inputs, [tiled_t(1)] + specs
    kept = jnp.bfloat16 if masked else jnp.float32
    pairs = rows * count * width
    return pl.pallas_call(
        partial(attend_back_kernel, heads, masked, old, (rows // TILE).bit_length() - 1),
        grid_spec=pltpu.PrefetchScalarGridSpec(
            num_scalar_prefetch=1,
            grid=(rows // TILE,),
            in_specs=specs,
            out_specs=[
                tiled_t(width) if old else tiled(width, 0),
                entire(count, width, 0),
                entire(count, width, 0),
            ],
            scratch_shapes=[
                pltpu.VMEM((count, width), jnp.float32),
                pltpu.VMEM((count, width), jnp.float32),
                pltpu.VMEM((width, TILE), jnp.float32),
            ],
        ),
        out_shape=[
            jax.ShapeDtypeStruct((width, rows), jnp.float32)
            if old
            else jax.ShapeDtypeStruct((rows, width), jnp.bfloat16),
            jax.ShapeDtypeStruct((count, width), kept),
            jax.ShapeDtypeStruct((count, width), kept),
        ],
        compiler_params=pltpu.CompilerParams(vmem_limit_bytes=VMEM),
        cost_estimate=pl.CostEstimate(
            flops=80 * pairs, bytes_accessed=4 * (rows + count) * width * 2, transcendentals=0
        ),
    )(meta, *inputs)


def layer_norm(value, gain, shift_by):
    centre = value - jnp.mean(value, axis=-1, keepdims=True)
    rstd = lax.rsqrt(jnp.mean(centre * centre, axis=-1, keepdims=True) + EPSILON)
    normed = centre * rstd
    return (normed * gain + shift_by, normed, rstd)


def norm_back(grad_out, normed, rstd, gain):
    scaled = grad_out * gain
    inner = scaled - jnp.mean(scaled, axis=-1, keepdims=True)
    inner = inner - normed * jnp.mean(scaled * normed, axis=-1, keepdims=True)
    return (rstd * inner, jnp.sum(grad_out * normed, axis=0), jnp.sum(grad_out, axis=0))


def gelu_and_slope(value):
    phi = 0.5 * (1.0 + lax.erf(value * 0.7071067811865476))
    bell = jnp.exp(-0.5 * value * value) * 0.3989422804014327
    return value * phi, phi + value * bell


def column_sum(value):
    return jnp.sum(wide(value), axis=0)


def per_device(
    inputs,
    encoded,
    doc_lengths,
    cotangent,
    query_weight,
    key_weight,
    value_weight,
    out_weight,
    memory_query,
    memory_key,
    memory_value,
    memory_out,
    up_weight,
    down_weight,
    query_bias,
    value_bias,
    memory_qbias,
    memory_vbias,
    up_bias,
    out_bias,
    memory_obias,
    down_bias,
    gain_self,
    shift_self,
    gain_memory,
    shift_memory,
    gain_dense,
    shift_dense,
):
    tp_index = lax.axis_index("tp")
    share_rows = inputs.shape[1]
    rows = share_rows * lax.axis_size("tp")
    width = query_weight.shape[1]
    base = lax.axis_index("ctx") * rows
    row_steps = steps_of("tp")
    weight_steps = steps_of("shard", "ctx")
    features = ("shard", "ctx")

    def turned(array, dim):
        return to_tree(array, dim, features, weight_steps)

    def turned_back(array, dim):
        return from_tree(array, dim, features, weight_steps)

    def gather_rows(piece):
        return gather_tree(piece, row_steps)

    def scatter_rows(make):
        return scatter_tree(make, rows, row_steps)

    def own_half(weight):
        part = weight.shape[0] // lax.axis_size("ctx")
        return lax.dynamic_slice_in_dim(weight, lax.axis_index("ctx") * part, part, 0)

    ctx_steps = steps_of("ctx")
    far_steps, near_steps = steps_of("shard")[:-1], steps_of("shard")[-1:]
    share = turned(inputs[0], 1)
    old_share = turned(shift(inputs[0], "ctx", 1), 1)
    inputs_rows = gather_rows(share)
    old_rows = gather_rows(old_share)
    qkv_own = own_half(jnp.concatenate([query_weight, key_weight, value_weight], axis=1))
    qkv_far = gather_tree(qkv_own, far_steps)
    qkv_near = gather_tree(qkv_far, near_steps)
    qkv_full = gather_tree(qkv_near, ctx_steps)
    out_far = gather_tree(own_half(out_weight.T), far_steps, qkv_far)
    out_near = gather_tree(out_far, near_steps, qkv_near)
    small_own = jnp.concatenate([memory_key, memory_value, memory_query, memory_out.T], axis=1)
    small_far = gather_tree(own_half(small_own), far_steps, qkv_near)
    small_near = gather_tree(small_far, near_steps)
    up_own = own_half(up_weight)
    down_own = own_half(down_weight.T)
    states = to_tree(turned(encoded[0], 1), 0, ("tp",), row_steps)
    vectors = turned(
        jnp.stack(
            [
                out_bias,
                memory_obias,
                down_bias,
                gain_self,
                shift_self,
                gain_memory,
                shift_memory,
                gain_dense,
                shift_dense,
            ]
        ),
        1,
    )
    (
        out_bias,
        memory_obias,
        down_bias,
        gain_self,
        shift_self,
        gain_memory,
        shift_memory,
        gain_dense,
        shift_dense,
    ) = [vectors[i] for i in range(9)]
    upstream = wide(turned(cotangent[0], 1))

    ends = jnp.cumsum(doc_lengths[0], dtype=jnp.int32)
    masks = jnp.asarray(masks_of(("tp",), row_steps), jnp.int32)
    starts = (masks ^ tp_index) * share_rows
    place = base + (starts[:, None] + jnp.arange(share_rows, dtype=jnp.int32)).reshape(-1)
    opens = jnp.max(jnp.where(place[:, None] >= ends[None, :], ends[None, :], 0), axis=1)
    lower = jnp.maximum(opens, place - (W - 1)) - base
    least = lower.reshape(-1, TILE)[:, 0] // TILE
    meta = jnp.concatenate([tp_index[None].astype(jnp.int32), least])
    lower = lower[None, :]

    zeros = jnp.zeros_like(query_bias)
    qkv = low(
        (matmul(inputs_rows, qkv_full) + jnp.concatenate([query_bias, zeros, value_bias]))
        * jnp.concatenate([zeros + 0.125, zeros + 1.0, zeros + 1.0])
    )
    old_kv = low(matmul(old_rows, qkv_full[:, width:]) + jnp.concatenate([zeros, value_bias]))
    qkv = after(qkv, out_near, small_near)
    mixed, mixed_t, self_lse = attend(
        meta, lower, (qkv, 0), (qkv, 1), (qkv, 2), width, (old_kv, None)
    )
    out_full = gather_tree(out_near, ctx_steps, qkv_full, mixed)
    mkv_full = gather_tree(small_near[:, : 2 * width], ctx_steps, old_kv, mixed)
    up_far = gather_tree(up_own, far_steps, small_near, mixed)
    mixed = after(mixed, mkv_full)
    attn_part = scatter_tree(
        lambda s: contract("rk,dk->rd", mixed[s], out_full), rows, row_steps[-1:]
    )

    mkv_own = low(
        matmul(states, after(mkv_full, attn_part)) + jnp.concatenate([zeros, memory_vbias])
    )

    def weight_terms(*pairs):
        def make(s):
            return jnp.concatenate(
                [contract("rd,rk->dk", left[:, s], right) for left, right in pairs], axis=1
            )

        return make

    model = share.shape[1]

    still = jnp.zeros((1,), jnp.int32)
    attn_share = scatter_more(attn_part, row_steps[:-1])
    first, normed_one, rstd_one = layer_norm(
        wide(share) + attn_share + out_bias, gain_self, shift_self
    )
    first_low = after(low(first), up_far)
    mkv = gather_tree(mkv_own, ctx_steps, None, first_low)
    up_near = gather_tree(up_far, near_steps, attn_part, first_low)
    down_far = gather_tree(down_own, far_steps, attn_part, first_low)
    small_full = gather_tree(small_near[:, 2 * width :], ctx_steps, attn_part, first_low)
    mquery_full, mout_full = small_full[:, :width], small_full[:, width:]
    first_rows = after(gather_rows(first_low), up_near, down_far)
    mquery = low((matmul(first_rows, mquery_full) + memory_qbias) * 0.125)
    cross_mixed, cross_mixed_t, cross_lse = attend(
        still, None, (mquery, 0), (mkv, 0), (mkv, 1), width
    )
    up_full = gather_tree(up_near, ctx_steps, mkv, cross_mixed)
    down_near = gather_tree(down_far, near_steps, mkv, cross_mixed)
    cross_mixed = after(cross_mixed, up_full, down_near)
    cross_share = scatter_rows(lambda s: contract("rk,dk->rd", cross_mixed[s], mout_full))
    second, normed_two, rstd_two = layer_norm(
        first + cross_share + memory_obias, gain_memory, shift_memory
    )
    second_low = low(second)
    down_full = gather_tree(down_near, ctx_steps, cross_mixed, second_low)
    second_rows = gather_rows(second_low)
    act, slope = gelu_and_slope(matmul(second_rows, up_full) + up_bias)
    act_low, slope_low = low(act), low(slope)
    dense_share = scatter_rows(lambda s: contract("rf,df->rd", act_low[s], down_full))
    result, normed_three, rstd_three = layer_norm(
        second + dense_share + down_bias, gain_dense, shift_dense
    )
    grad_three, gain_dense_grad, shift_dense_grad = norm_back(
        upstream, normed_three, rstd_three, gain_dense
    )
    dense_low = low(grad_three)
    dense_rows = gather_rows(dense_low)
    hidden_low = low(matmul(dense_rows, down_full) * wide(slope_low))
    second_share = scatter_rows(lambda s: contract("rf,df->rd", hidden_low[s], up_full))
    grad_two, gain_memory_grad, shift_memory_grad = norm_back(
        grad_three + second_share, normed_two, rstd_two, gain_memory
    )

    cross_low = low(grad_two)
    down_part = scatter_tree(weight_terms((dense_rows, act_low)), model, ctx_steps, cross_low)
    cross_rows = gather_rows(cross_low)
    down_near_grad = scatter_more(down_part, near_steps, None, cross_rows)
    grad_cross_mixed = low(matmul(cross_rows, mout_full))
    mquery_back, mkeys_back, mvalues_back = attend_back(
        still,
        None,
        (mquery, 0),
        grad_cross_mixed,
        cross_mixed_t,
        cross_lse,
        (mkv, 0),
        (mkv, 1),
        width,
        "cross",
    )
    mquery_pre = mquery_back * 0.125
    down_grads = scatter_more(down_near_grad, far_steps, None, mquery_pre)
    up_part = scatter_tree(weight_terms((second_rows, hidden_low)), model, ctx_steps, mquery_pre)
    first_part = scatter_tree(
        lambda s: contract("rk,dk->rd", mquery_pre[s], mquery_full), rows, row_steps[-1:]
    )
    first_share = scatter_more(first_part, row_steps[:-1])
    grad_one, gain_self_grad, shift_self_grad = norm_back(
        grad_two + first_share, normed_one, rstd_one, gain_self
    )
    self_low = low(grad_one)
    self_rows = gather_rows(self_low)
    up_near_grad = scatter_more(up_part, near_steps, first_part, self_low)
    up_grads = scatter_more(up_near_grad, far_steps, None, self_rows)
    mkv_back = after(jnp.concatenate([mkeys_back, mvalues_back], axis=1), first_part)
    mkv_low = low(scatter_tree(lambda s: mkv_back[s], mkv_back.shape[0], ctx_steps))
    encoded_grad = scatter_tree(
        lambda s: contract("ek,dk->ed", mkv_low[s], mkv_full), states.shape[0], row_steps
    )
    small_part = scatter_tree(
        weight_terms((states, mkv_low), (first_rows, mquery_pre), (cross_rows, cross_mixed)),
        model,
        ctx_steps,
        self_rows,
    )
    grad_self = after(low(matmul(self_rows, out_full)), small_part)

    query_start, old_keys, old_values = attend_back(
        meta,
        lower,
        (qkv, 0),
        grad_self,
        mixed_t,
        self_lse,
        (old_kv, 0),
        (old_kv, 1),
        width,
        "old",
    )
    old_back = jnp.concatenate([old_keys, old_values], axis=1)
    back = shift(old_back, "ctx", -1)
    small_near_grads = scatter_more(small_part, near_steps, None, old_back)
    grad_self_later = after(grad_self, small_near_grads, query_start)
    query_back, keys_back, values_back = attend_back(
        meta,
        lower,
        (qkv, 0),
        grad_self_later,
        mixed_t,
        self_lse,
        (qkv, 1),
        (qkv, 2),
        width,
        "own",
        query_start,
    )
    query_pre = query_back * 0.125
    small_grads = scatter_more(small_near_grads, far_steps, None, query_pre)
    out_part = scatter_tree(weight_terms((self_rows, mixed)), model, ctx_steps, query_pre)
    own_back = jnp.concatenate([query_pre, keys_back, values_back], axis=1)

    def qkv_terms(s):
        own = contract("rd,rk->dk", inputs_rows[:, s], own_back)
        old = contract("rd,rk->dk", old_rows[:, s], old_back)
        return own + jnp.pad(old, ((0, 0), (width, 0)))

    kv_all = low(wide(own_back[:, width:]) + wide(back))

    def inputs_term(s):
        term = contract("rk,dk->rd", query_pre[s], qkv_full[:, :width])
        return term + contract("rk,dk->rd", kv_all[s], qkv_full[:, width:])

    inputs_part = scatter_tree(inputs_term, rows, row_steps[-1:])
    inputs_grad = grad_one + scatter_more(inputs_part, row_steps[:-1])
    qkv_grads = scatter_more(
        scatter_tree(qkv_terms, model, ctx_steps, inputs_part), weight_steps[: -len(ctx_steps)]
    )
    out_grads = scatter_more(out_part, steps_of("shard"), inputs_part)

    everywhere = jnp.stack(
        [
            column_sum(self_low),
            column_sum(cross_low),
            column_sum(dense_low),
            gain_self_grad,
            shift_self_grad,
            gain_memory_grad,
            shift_memory_grad,
            gain_dense_grad,
            shift_dense_grad,
        ]
    )
    everywhere = all_sum(turned_back(everywhere, 1), row_steps)
    by_heads = jnp.concatenate(
        [
            column_sum(query_pre),
            column_sum(values_back) + column_sum(old_values),
            column_sum(mquery_pre),
            column_sum(mkv_low[:, width:]),
            column_sum(hidden_low),
        ]
    )
    lanes = 128
    sums = all_sum(
        after(
            jnp.concatenate([everywhere.reshape(-1, lanes), by_heads.reshape(-1, lanes)], axis=0),
            inputs_part,
        ),
        weight_steps,
    )
    cut = everywhere.size // lanes
    totals = sums[:cut].reshape(everywhere.shape)
    head_totals = sums[cut:].reshape(-1)
    return (
        turned_back(low(result), 1)[None],
        turned_back(inputs_grad, 1)[None],
        turned_back(encoded_grad, 1)[None],
        qkv_grads[:, :width],
        qkv_grads[:, width : 2 * width],
        qkv_grads[:, 2 * width :],
        out_grads.T,
        small_grads[:, 2 * width : 3 * width],
        small_grads[:, :width],
        small_grads[:, width : 2 * width],
        small_grads[:, 3 * width :].T,
        up_grads,
        down_grads.T,
        head_totals[:width],
        head_totals[width : 2 * width],
        head_totals[2 * width : 3 * width],
        head_totals[3 * width : 4 * width],
        head_totals[4 * width :],
        totals[0],
        totals[1],
        totals[2],
        totals[3],
        totals[4],
        totals[5],
        totals[6],
        totals[7],
        totals[8],
    )


def solution(mesh):
    placed = (
        P("shard", ("ctx", "tp"), None),
        P("shard", "ctx", None),
        P("shard", None),
        P("shard", ("ctx", "tp"), None),
        P("shard", "tp"),
        P("shard", "tp"),
        P("shard", "tp"),
        P("tp", "shard"),
        P("shard", "tp"),
        P("shard", "tp"),
        P("shard", "tp"),
        P("tp", "shard"),
        P("shard", "tp"),
        P("tp", "shard"),
        P("tp"),
        P("tp"),
        P("tp"),
        P("tp"),
        P("tp"),
        P(),
        P(),
        P(),
        P(),
        P(),
        P(),
        P(),
        P(),
        P(),
    )
    return jax.shard_map(
        per_device,
        mesh=mesh,
        in_specs=placed,
        out_specs=(
            P("shard", ("ctx", "tp"), None),
            P("shard", ("ctx", "tp"), None),
            P("shard", ("ctx", "tp"), None),
            P(("shard", "ctx"), "tp"),
            P(("shard", "ctx"), "tp"),
            P(("shard", "ctx"), "tp"),
            P("tp", ("shard", "ctx")),
            P(("shard", "ctx"), "tp"),
            P(("shard", "ctx"), "tp"),
            P(("shard", "ctx"), "tp"),
            P("tp", ("shard", "ctx")),
            P(("shard", "ctx"), "tp"),
            P("tp", ("shard", "ctx")),
            P("tp"),
            P("tp"),
            P("tp"),
            P("tp"),
            P("tp"),
            P(),
            P(),
            P(),
            P(),
            P(),
            P(),
            P(),
            P(),
            P(),
        ),
        check_vma=False,
    )
```

```python
from functools import partial

import jax
import jax.numpy as jnp
from jax import lax
from jax.experimental import pallas as pl
from jax.experimental.pallas import tpu as pltpu
from jax.sharding import PartitionSpec as P

HDIM = 64
W = 1024
TILE = 256


EPSILON = 1e-05
NEGATIVE = -1e30
VMEM = 32 * 1024 * 1024


def matmul(left, right):
    return jnp.dot(left, right, preferred_element_type=jnp.float32)


def contract(form, left, right):
    return jnp.einsum(form, left, right, preferred_element_type=jnp.float32)


def low(value):
    return value.astype(jnp.bfloat16)


def wide(value):
    return value.astype(jnp.float32)


def swap(array, axis, bit):
    return lax.ppermute(array, axis, [(i, i ^ bit) for i in range(lax.axis_size(axis))])


def shift(array, axis, by):
    count = lax.axis_size(axis)
    pairs = [(i, i + by) for i in range(count) if 0 <= i + by < count]
    return lax.ppermute(array, axis, pairs)


def steps_of(*axes):
    steps = []
    for axis in axes:
        bit = lax.axis_size(axis) // 2
        while bit:
            steps.append((axis, bit))
            bit //= 2
    return steps


def after(value, *others):
    others = [other for other in others if other is not None]
    return lax.optimization_barrier((value, *others))[0] if others else value


def gather_tree(array, steps, start=None, used=None):
    for n, (axis, bit) in enumerate(steps):
        arrived = swap(after(array, start if n == 0 else None), axis, bit)
        array = jnp.concatenate([after(array, used if n == len(steps) - 1 else None), arrived])
    return array


def scatter_more(total, steps, start=None, used=None):
    for n, (axis, bit) in enumerate(reversed(steps)):
        half = total.shape[0] // 2
        arrived = swap(after(low(total[half:]), start if n == 0 else None), axis, bit)
        kept = after(total[:half], used if n == len(steps) - 1 else None)
        total = kept + wide(arrived)
    return total


def scatter_tree(make, size, steps, used=None):
    axis, bit = steps[-1]
    half = size // 2
    arrived = swap(low(make(slice(half, size))), axis, bit)
    total = after(make(slice(0, half)), used) + wide(arrived)
    return scatter_more(total, steps[:-1])


def all_sum(value, steps):
    for axis, bit in steps:
        value = value + swap(value, axis, bit)
    return value


def flat_bit(step, axes):
    axis, bit = step
    for other in axes[axes.index(axis) + 1 :]:
        bit = bit * lax.axis_size(other)
    return bit


def masks_of(axes, steps):
    masks = [0]
    for step in steps:
        masks = masks + [m | flat_bit(step, axes) for m in masks]
    return masks


def cross_over(blocks, axes):
    index = lax.axis_index(axes)
    bit = 1
    while bit < len(blocks):
        odd = (index & bit) != 0
        blocks = [jnp.where(odd, blocks[m ^ bit], blocks[m]) for m in range(len(blocks))]
        bit *= 2
    return blocks


def split(array, dim, count):
    size = array.shape[dim] // count
    return [lax.slice_in_dim(array, m * size, (m + 1) * size, axis=dim) for m in range(count)]


def to_tree(array, dim, axes, steps):
    masks = masks_of(axes, steps)
    blocks = cross_over(split(array, dim, len(masks)), axes)
    return jnp.concatenate([blocks[m] for m in masks], axis=dim)


def from_tree(array, dim, axes, steps):
    masks = masks_of(axes, steps)
    blocks = split(array, dim, len(masks))
    blocks = cross_over([blocks[masks.index(m)] for m in range(len(masks))], axes)
    return jnp.concatenate(blocks, axis=dim)


def in_tree(block, bits):
    return sum(((block >> k) & 1) << (bits - 1 - k) for k in range(bits))


def stack_heads(value, heads, turned):
    feature = lax.broadcasted_iota(jnp.int32, value.shape, 0 if turned else 1) // HDIM
    zero = jnp.zeros_like(value)
    parts = [jnp.where(feature == h, value, zero) for h in range(heads)]
    return jnp.concatenate(parts, axis=1 if turned else 0)


def allowed_in(lower, query, key_start, count):
    key = key_start + lax.broadcasted_iota(jnp.int32, (count, lower.shape[1]), 0)
    return (key >= lower) & (key <= query)


def along_heads(row, heads):
    return jnp.concatenate([row] * heads, axis=1)


def tile_of(ref, index, count, columns=None):
    rows = pl.ds(pl.multiple_of(index * count, count), count)
    return ref[rows, :] if columns is None else ref[rows, columns]


def lanes_of(index, count):
    return pl.ds(pl.multiple_of(index * count, count), count)


def attend_kernel(width, masked, *refs):
    if masked:
        meta, lower_ref, source_ref, old_ref, mixed_ref, mixed_t_ref, lse_ref, acc_ref = refs
        query_ref, first = source_ref, width
    else:
        query_ref, source_ref, mixed_ref, mixed_t_ref, lse_ref, acc_ref = refs
        first = 0
    heads, count = width // HDIM, TILE
    steps = mixed_ref.shape[0] // count
    bits = steps.bit_length() - 1

    @pl.loop(0, steps)
    def _(step):
        stacked = stack_heads(tile_of(query_ref, step, count, slice(0, width)).T, heads, True)
        acc_ref[...] = jnp.zeros_like(acc_ref)
        if masked:
            tile = in_tree(step, bits) ^ meta[0]
            lower = along_heads(lower_ref[:, lanes_of(step, count)], heads)
            place_of = tile * count + lax.broadcasted_iota(jnp.int32, (1, count), 1)
            place_of = along_heads(place_of, heads)

        def add(carry, ref, column, place, key_tile, masking, size=count):
            keys = tile_of(ref, place, size, slice(column, column + width))
            values_t = tile_of(ref, place, size, slice(column + width, column + 2 * width)).T
            top, total = carry
            scores = matmul(keys, stacked)
            if masking:
                ok = allowed_in(lower, place_of, key_tile * count, count)
                scores = jnp.where(ok, scores, NEGATIVE)
            higher = jnp.maximum(top, jnp.max(scores, axis=0, keepdims=True))
            expo = jnp.exp(scores - higher)
            scale = jnp.exp(top - higher)
            total = total * scale + jnp.sum(expo, axis=0, keepdims=True)
            expo = low(expo)
            for h in range(heads):
                part, lanes = slice(h * HDIM, (h + 1) * HDIM), slice(h * count, (h + 1) * count)
                acc_ref[part, :] = acc_ref[part, :] * scale[:, lanes] + matmul(
                    values_t[part, :], expo[:, lanes]
                )
            return higher, total

        carry = (
            jnp.full((1, heads * count), NEGATIVE, jnp.float32),
            jnp.zeros((1, heads * count), jnp.float32),
        )
        if masked:
            least = meta[1 + step]
            here = lambda n, c: add(
                c, source_ref, first, in_tree((tile - n) ^ meta[0], bits), tile - n, True
            )
            carry = lax.fori_loop(0, tile - jnp.maximum(least, 0) + 1, here, carry)
            before = lambda n, c: add(
                c, old_ref, 0, in_tree((n + steps) ^ meta[0], bits), n, True
            )
            carry = lax.fori_loop(least, 0, before, carry)
        else:
            every = lambda n, c: add(c, source_ref, first, n, n, False, 2 * count)
            carry = lax.fori_loop(0, source_ref.shape[0] // (2 * count), every, carry)
        top, total = carry
        lse = top + jnp.log(total)
        whole = lanes_of(step, count)
        for h in range(heads):
            part, lanes = slice(h * HDIM, (h + 1) * HDIM), slice(h * count, (h + 1) * count)
            acc_ref[part, :] = acc_ref[part, :] / total[:, lanes]
            lse_ref[h : h + 1, whole] = lse[:, lanes]
        mixed_t_ref[:, whole] = acc_ref[...]
        mixed_ref[whole, :] = low(acc_ref[...].T)


def attend_back_kernel(width, kind, *refs):
    refs = list(refs)
    masked, old = kind != "cross", kind == "old"
    if masked:
        meta, lower_ref = refs.pop(0), refs.pop(0)
    start_ref = refs.pop(0) if kind == "own" else None
    query_ref = refs.pop(0)
    grad_ref, mixed_t_ref, lse_ref = refs[:3]
    refs = refs[3:]
    source_ref = query_ref if kind == "own" else refs.pop(0)
    first = width if kind == "own" else 0
    grad_query_ref, grad_kv_ref, keys_acc, values_acc, query_acc = refs
    heads, count = width // HDIM, TILE
    steps = grad_ref.shape[0] // count
    bits = steps.bit_length() - 1
    keys_acc[...] = jnp.zeros_like(keys_acc)
    values_acc[...] = jnp.zeros_like(values_acc)

    def of_queries(step):
        whole = lanes_of(step, count)
        query = tile_of(query_ref, step, count, slice(0, width))
        grad = tile_of(grad_ref, step, count)
        grad_t = grad.T
        stacked = stack_heads(query, heads, False)
        stacked_t = stack_heads(query.T, heads, True)
        stacked_grad = stack_heads(grad, heads, False)
        stacked_grad_t = stack_heads(grad_t, heads, True)
        weighed = wide(grad_t) * mixed_t_ref[:, whole]
        lse = jnp.concatenate([lse_ref[h : h + 1, whole] for h in range(heads)], axis=1)
        inner = jnp.concatenate(
            [
                jnp.sum(weighed[h * HDIM : (h + 1) * HDIM, :], axis=0, keepdims=True)
                for h in range(heads)
            ],
            axis=1,
        )
        if masked:
            tile = in_tree(step, bits) ^ meta[0]
            lower = along_heads(lower_ref[:, whole], heads)
            place_of = tile * count + lax.broadcasted_iota(jnp.int32, (1, count), 1)
            place_of = along_heads(place_of, heads)

        def add(place, key_tile, size=count):
            rows = pl.ds(pl.multiple_of(place * size, size), size)
            keys = source_ref[rows, first : first + width]
            values = source_ref[rows, first + width : first + 2 * width]
            keys_t = keys.T
            probs = jnp.exp(matmul(keys, stacked_t) - lse)
            if masked:
                ok = allowed_in(lower, place_of, key_tile * count, count)
                probs = jnp.where(ok, probs, 0.0)
            slopes = low(probs * (matmul(values, stacked_grad_t) - inner))
            values_acc[rows, :] += matmul(low(probs), stacked_grad)
            keys_acc[rows, :] += matmul(slopes, stacked)
            for h in range(heads):
                part, lanes = slice(h * HDIM, (h + 1) * HDIM), slice(h * count, (h + 1) * count)
                query_acc[part, :] += matmul(keys_t[part, :], slopes[:, lanes])

        if not masked:
            pl.loop(0, source_ref.shape[0] // (2 * count))(lambda n: add(n, n, 2 * count))
        elif old:
            pl.loop(meta[1 + step], 0)(lambda n: add(in_tree((n + steps) ^ meta[0], bits), n))
        else:
            pl.loop(jnp.maximum(meta[1 + step], 0), tile + 1)(
                lambda n: add(in_tree(n ^ meta[0], bits), n)
            )

    @pl.loop(0, steps)
    def _(step):
        whole = lanes_of(step, count)
        if start_ref is None:
            query_acc[...] = jnp.zeros_like(query_acc)
        else:
            query_acc[...] = start_ref[:, whole]
        if old:
            pl.when(meta[1 + step] < 0)(lambda: of_queries(step))
            grad_query_ref[:, whole] = query_acc[...]
        else:
            of_queries(step)
            grad_query_ref[whole, :] = low(query_acc[...].T)

    grad_kv_ref[:, :width] = keys_acc[...].astype(grad_kv_ref.dtype)
    grad_kv_ref[:, width:] = values_acc[...].astype(grad_kv_ref.dtype)


IN_VMEM = pl.BlockSpec(memory_space=pltpu.VMEM)
IN_SMEM = pl.BlockSpec(memory_space=pltpu.SMEM)


def attend(width, query, source, meta=None, lower=None, old=None):
    rows = query.shape[0]
    heads = width // HDIM
    masked = old is not None
    inputs = [meta, lower, source, old] if masked else [query, source]
    specs = [IN_SMEM if masked else IN_VMEM] + [IN_VMEM] * (len(inputs) - 1)
    pairs = rows * source.shape[0] * width
    return pl.pallas_call(
        partial(attend_kernel, width, masked),
        in_specs=specs,
        out_specs=[IN_VMEM] * 3,
        out_shape=[
            jax.ShapeDtypeStruct((rows, width), jnp.bfloat16),
            jax.ShapeDtypeStruct((width, rows), jnp.float32),
            jax.ShapeDtypeStruct((heads, rows), jnp.float32),
        ],
        scratch_shapes=[pltpu.VMEM((width, TILE), jnp.float32)],
        compiler_params=pltpu.CompilerParams(vmem_limit_bytes=VMEM),
        cost_estimate=pl.CostEstimate(
            flops=48 * pairs, bytes_accessed=8 * rows * width, transcendentals=0
        ),
    )(*inputs)


def attend_back(width, kind, query, grad, mixed_t, lse, source=None, meta=None, lower=None, start=None):
    rows = grad.shape[0]
    inputs = [] if kind == "cross" else [meta, lower]
    inputs += [start] if kind == "own" else []
    inputs += [query, grad, mixed_t, lse] + ([] if kind == "own" else [source])
    specs = [IN_VMEM] * len(inputs)
    if kind != "cross":
        specs[0] = IN_SMEM
    count = (query if kind == "own" else source).shape[0]
    pairs = rows * count * width
    return pl.pallas_call(
        partial(attend_back_kernel, width, kind),
        in_specs=specs,
        out_specs=[IN_VMEM] * 2,
        out_shape=[
            jax.ShapeDtypeStruct((width, rows), jnp.float32)
            if kind == "old"
            else jax.ShapeDtypeStruct((rows, width), jnp.bfloat16),
            jax.ShapeDtypeStruct(
                (count, 2 * width), jnp.float32 if kind == "cross" else jnp.bfloat16
            ),
        ],
        scratch_shapes=[
            pltpu.VMEM((count, width), jnp.float32),
            pltpu.VMEM((count, width), jnp.float32),
            pltpu.VMEM((width, TILE), jnp.float32),
        ],
        compiler_params=pltpu.CompilerParams(vmem_limit_bytes=VMEM),
        cost_estimate=pl.CostEstimate(
            flops=64 * pairs, bytes_accessed=16 * rows * width, transcendentals=0
        ),
    )(*inputs)


def layer_norm(value, gain, shift_by):
    centre = value - jnp.mean(value, axis=-1, keepdims=True)
    rstd = lax.rsqrt(jnp.mean(centre * centre, axis=-1, keepdims=True) + EPSILON)
    normed = centre * rstd
    return (normed * gain + shift_by, normed, rstd)


def norm_back(grad_out, normed, rstd, gain):
    scaled = grad_out * gain
    inner = scaled - jnp.mean(scaled, axis=-1, keepdims=True)
    inner = inner - normed * jnp.mean(scaled * normed, axis=-1, keepdims=True)
    return (rstd * inner, jnp.sum(grad_out * normed, axis=0), jnp.sum(grad_out, axis=0))


def gelu_and_slope(value):
    phi = 0.5 * (1.0 + lax.erf(value * 0.7071067811865476))
    bell = jnp.exp(-0.5 * value * value) * 0.3989422804014327
    return value * phi, phi + value * bell


def column_sum(value):
    return jnp.sum(wide(value), axis=0)


def per_device(
    inputs,
    encoded,
    doc_lengths,
    cotangent,
    query_weight,
    key_weight,
    value_weight,
    out_weight,
    memory_query,
    memory_key,
    memory_value,
    memory_out,
    up_weight,
    down_weight,
    query_bias,
    value_bias,
    memory_qbias,
    memory_vbias,
    up_bias,
    out_bias,
    memory_obias,
    down_bias,
    gain_self,
    shift_self,
    gain_memory,
    shift_memory,
    gain_dense,
    shift_dense,
):
    tp_index = lax.axis_index("tp")
    share_rows = inputs.shape[1]
    rows = share_rows * lax.axis_size("tp")
    width = query_weight.shape[1]
    base = lax.axis_index("ctx") * rows
    row_steps = steps_of("tp")
    weight_steps = steps_of("shard", "ctx")
    features = ("shard", "ctx")

    def turned(array, dim):
        return to_tree(array, dim, features, weight_steps)

    def turned_back(array, dim):
        return from_tree(array, dim, features, weight_steps)

    def gather_rows(piece):
        return gather_tree(piece, row_steps)

    def scatter_rows(make):
        return scatter_tree(make, rows, row_steps)

    def own_half(weight):
        part = weight.shape[0] // lax.axis_size("ctx")
        return lax.dynamic_slice_in_dim(weight, lax.axis_index("ctx") * part, part, 0)

    ctx_steps = steps_of("ctx")
    far_steps, near_steps = steps_of("shard")[:-1], steps_of("shard")[-1:]
    share = turned(inputs[0], 1)
    old_share = turned(shift(inputs[0], "ctx", 1), 1)
    inputs_rows = gather_rows(share)
    old_rows = gather_rows(old_share)
    qkv_own = own_half(jnp.concatenate([query_weight, key_weight, value_weight], axis=1))
    qkv_far = gather_tree(qkv_own, far_steps)
    qkv_near = gather_tree(qkv_far, near_steps)
    qkv_full = gather_tree(qkv_near, ctx_steps)
    out_far = gather_tree(own_half(out_weight.T), far_steps, qkv_far)
    out_near = gather_tree(out_far, near_steps, qkv_near)
    small_own = jnp.concatenate([memory_key, memory_value, memory_query, memory_out.T], axis=1)
    small_far = gather_tree(own_half(small_own), far_steps, qkv_near)
    up_own = own_half(up_weight)
    down_own = own_half(down_weight.T)
    states = to_tree(turned(encoded[0], 1), 0, ("tp",), row_steps)
    vectors = turned(
        jnp.stack(
            [
                out_bias,
                memory_obias,
                down_bias,
                gain_self,
                shift_self,
                gain_memory,
                shift_memory,
                gain_dense,
                shift_dense,
            ]
        ),
        1,
    )
    (
        out_bias,
        memory_obias,
        down_bias,
        gain_self,
        shift_self,
        gain_memory,
        shift_memory,
        gain_dense,
        shift_dense,
    ) = [vectors[i] for i in range(9)]
    upstream = wide(turned(cotangent[0], 1))

    ends = jnp.cumsum(doc_lengths[0], dtype=jnp.int32)
    masks = jnp.asarray(masks_of(("tp",), row_steps), jnp.int32)
    starts = (masks ^ tp_index) * share_rows
    place = base + (starts[:, None] + jnp.arange(share_rows, dtype=jnp.int32)).reshape(-1)
    opens = jnp.max(jnp.where(place[:, None] >= ends[None, :], ends[None, :], 0), axis=1)
    lower = jnp.maximum(opens, place - (W - 1)) - base
    least = lower.reshape(-1, TILE)[:, 0] // TILE
    meta = jnp.concatenate([tp_index[None].astype(jnp.int32), least])
    lower = lower[None, :]

    zeros = jnp.zeros_like(query_bias)
    qkv = low(
        (matmul(inputs_rows, qkv_full) + jnp.concatenate([query_bias, zeros, value_bias]))
        * jnp.concatenate([zeros + 0.125, zeros + 1.0, zeros + 1.0])
    )
    old_kv = low(matmul(old_rows, qkv_full[:, width:]) + jnp.concatenate([zeros, value_bias]))
    small_near = gather_tree(small_far, near_steps, None, qkv)
    qkv = after(qkv, out_near, small_near)
    mixed, mixed_t, self_lse = attend(width, qkv, qkv, meta, lower, old_kv)
    out_full = gather_tree(out_near, ctx_steps, qkv_full, mixed)
    mkv_full = gather_tree(small_near[:, : 2 * width], ctx_steps, None, mixed)
    up_far = gather_tree(up_own, far_steps, small_near, mixed)
    mixed = after(mixed, mkv_full, up_far)
    attn_part = scatter_tree(
        lambda s: contract("rk,dk->rd", mixed[s], out_full), rows, row_steps[-1:]
    )

    mkv_own = low(
        matmul(states, after(mkv_full, attn_part)) + jnp.concatenate([zeros, memory_vbias])
    )

    def weight_terms(*pairs):
        def make(s):
            return jnp.concatenate(
                [contract("rd,rk->dk", left[:, s], right) for left, right in pairs], axis=1
            )

        return make

    model = share.shape[1]

    attn_share = scatter_more(attn_part, row_steps[:-1])
    first, normed_one, rstd_one = layer_norm(
        wide(share) + attn_share + out_bias, gain_self, shift_self
    )
    up_near = gather_tree(up_far, near_steps, mixed, attn_part)
    down_far = gather_tree(down_own, far_steps, mixed, attn_part)
    mkv = gather_tree(mkv_own, ctx_steps)
    small_full = gather_tree(small_near[:, 2 * width :], ctx_steps, mixed, attn_part)
    first_low = after(low(first), up_near, down_far, mkv, small_full)
    mquery_full, mout_full = small_full[:, :width], small_full[:, width:]
    first_rows = gather_rows(first_low)
    down_near = gather_tree(down_far, near_steps, first_low, first_rows)
    mquery = low((matmul(first_rows, mquery_full) + memory_qbias) * 0.125)
    mquery = after(mquery, down_near)
    cross_mixed, cross_mixed_t, cross_lse = attend(width, mquery, mkv)
    up_full = gather_tree(up_near, ctx_steps, first_low, cross_mixed)
    cross_part = scatter_tree(
        lambda s: contract("rk,dk->rd", cross_mixed[s], mout_full), rows, row_steps[-1:]
    )
    cross_part = after(cross_part, up_full)
    cross_share = scatter_more(cross_part, row_steps[:-1])
    second, normed_two, rstd_two = layer_norm(
        first + cross_share + memory_obias, gain_memory, shift_memory
    )
    second_low = low(second)
    down_full = gather_tree(down_near, ctx_steps, cross_part, second_low)
    second_rows = after(gather_rows(second_low), down_full)
    act, slope = gelu_and_slope(matmul(second_rows, up_full) + up_bias)
    act_low, slope_low = low(act), low(slope)
    dense_share = scatter_rows(lambda s: contract("rf,df->rd", act_low[s], down_full))
    result, normed_three, rstd_three = layer_norm(
        second + dense_share + down_bias, gain_dense, shift_dense
    )
    grad_three, gain_dense_grad, shift_dense_grad = norm_back(
        upstream, normed_three, rstd_three, gain_dense
    )
    dense_low = low(grad_three)
    dense_rows = gather_rows(dense_low)
    hidden_low = low(matmul(dense_rows, down_full) * wide(slope_low))
    second_share = scatter_rows(lambda s: contract("rf,df->rd", hidden_low[s], up_full))
    grad_two, gain_memory_grad, shift_memory_grad = norm_back(
        grad_three + second_share, normed_two, rstd_two, gain_memory
    )

    cross_low = low(grad_two)
    cross_rows = gather_rows(cross_low)
    down_part = scatter_tree(weight_terms((dense_rows, act_low)), model, ctx_steps, cross_rows)
    grad_cross_mixed = low(matmul(cross_rows, mout_full))
    mquery_back, mkv_sum = attend_back(
        width, "cross", mquery, grad_cross_mixed, cross_mixed_t, cross_lse, mkv
    )
    mquery_pre = mquery_back * 0.125
    down_near_grad = scatter_more(down_part, near_steps, None, mquery_pre)
    up_part = scatter_tree(weight_terms((second_rows, hidden_low)), model, ctx_steps, mquery_pre)
    first_part = scatter_tree(
        lambda s: contract("rk,dk->rd", mquery_pre[s], mquery_full), rows, row_steps[-1:]
    )
    first_share = scatter_more(first_part, row_steps[:-1])
    grad_one, gain_self_grad, shift_self_grad = norm_back(
        grad_two + first_share, normed_one, rstd_one, gain_self
    )
    self_low = low(grad_one)
    self_rows = gather_rows(self_low)
    down_grads = scatter_more(down_near_grad, far_steps, first_part, self_low)
    up_near_grad = scatter_more(up_part, near_steps, first_part, self_low)
    up_grads = scatter_more(up_near_grad, far_steps, None, self_rows)
    mkv_back = after(mkv_sum, first_part)
    mkv_low = low(scatter_tree(lambda s: mkv_back[s], mkv_back.shape[0], ctx_steps))
    encoded_grad = scatter_tree(
        lambda s: contract("ek,dk->ed", mkv_low[s], mkv_full), states.shape[0], row_steps
    )
    small_part = scatter_tree(
        weight_terms((states, mkv_low), (first_rows, mquery_pre), (cross_rows, cross_mixed)),
        model,
        ctx_steps,
        self_rows,
    )
    grad_self = after(low(matmul(self_rows, out_full)), small_part)

    query_start, old_back = attend_back(
        width, "old", qkv, grad_self, mixed_t, self_lse, old_kv, meta, lower
    )
    back = shift(old_back, "ctx", -1)
    small_near_grads = scatter_more(small_part, near_steps, None, old_back)
    grad_self_later = after(grad_self, small_near_grads, query_start)
    query_back, kv_back = attend_back(
        width, "own", qkv, grad_self_later, mixed_t, self_lse, None, meta, lower, query_start
    )
    query_pre = query_back * 0.125
    small_grads = scatter_more(small_near_grads, far_steps, None, query_pre)
    own_back = jnp.concatenate([query_pre, kv_back], axis=1)

    def qkv_terms(s):
        own = contract("rd,rk->dk", inputs_rows[:, s], own_back)
        old = contract("rd,rk->dk", old_rows[:, s], old_back)
        return own + jnp.pad(old, ((0, 0), (width, 0)))

    kv_all = low(wide(kv_back) + wide(back))

    def inputs_term(s):
        term = contract("rk,dk->rd", query_pre[s], qkv_full[:, :width])
        return term + contract("rk,dk->rd", kv_all[s], qkv_full[:, width:])

    inputs_part = scatter_tree(inputs_term, rows, row_steps[-1:])
    inputs_grad = grad_one + scatter_more(inputs_part, row_steps[:-1])
    sent = low(inputs_part[inputs_part.shape[0] // 2 :])
    qkv_grads = scatter_more(
        scatter_tree(qkv_terms, model, ctx_steps, sent), weight_steps[: -len(ctx_steps)]
    )
    out_part = scatter_tree(weight_terms((self_rows, mixed)), model, ctx_steps, sent)
    out_grads = scatter_more(out_part, steps_of("shard"))

    everywhere = jnp.stack(
        [
            column_sum(self_low),
            column_sum(cross_low),
            column_sum(dense_low),
            gain_self_grad,
            shift_self_grad,
            gain_memory_grad,
            shift_memory_grad,
            gain_dense_grad,
            shift_dense_grad,
        ]
    )
    everywhere = all_sum(turned_back(everywhere, 1), row_steps)
    by_heads = jnp.concatenate(
        [
            column_sum(query_pre),
            column_sum(kv_back[:, width:]) + column_sum(old_back[:, width:]),
            column_sum(mquery_pre),
            column_sum(mkv_low[:, width:]),
            column_sum(hidden_low),
        ]
    )
    lanes = 128
    sums = all_sum(
        after(
            jnp.concatenate([everywhere.reshape(-1, lanes), by_heads.reshape(-1, lanes)], axis=0),
            sent,
        ),
        weight_steps,
    )
    cut = everywhere.size // lanes
    totals = sums[:cut].reshape(everywhere.shape)
    head_totals = sums[cut:].reshape(-1)
    return (
        turned_back(low(result), 1)[None],
        turned_back(inputs_grad, 1)[None],
        turned_back(encoded_grad, 1)[None],
        qkv_grads[:, :width],
        qkv_grads[:, width : 2 * width],
        qkv_grads[:, 2 * width :],
        out_grads.T,
        small_grads[:, 2 * width : 3 * width],
        small_grads[:, :width],
        small_grads[:, width : 2 * width],
        small_grads[:, 3 * width :].T,
        up_grads,
        down_grads.T,
        head_totals[:width],
        head_totals[width : 2 * width],
        head_totals[2 * width : 3 * width],
        head_totals[3 * width : 4 * width],
        head_totals[4 * width :],
        totals[0],
        totals[1],
        totals[2],
        totals[3],
        totals[4],
        totals[5],
        totals[6],
        totals[7],
        totals[8],
    )


def solution(mesh):
    placed = (
        P("shard", ("ctx", "tp"), None),
        P("shard", "ctx", None),
        P("shard", None),
        P("shard", ("ctx", "tp"), None),
        P("shard", "tp"),
        P("shard", "tp"),
        P("shard", "tp"),
        P("tp", "shard"),
        P("shard", "tp"),
        P("shard", "tp"),
        P("shard", "tp"),
        P("tp", "shard"),
        P("shard", "tp"),
        P("tp", "shard"),
        P("tp"),
        P("tp"),
        P("tp"),
        P("tp"),
        P("tp"),
        P(),
        P(),
        P(),
        P(),
        P(),
        P(),
        P(),
        P(),
        P(),
    )
    return jax.shard_map(
        per_device,
        mesh=mesh,
        in_specs=placed,
        out_specs=(
            P("shard", ("ctx", "tp"), None),
            P("shard", ("ctx", "tp"), None),
            P("shard", ("ctx", "tp"), None),
            P(("shard", "ctx"), "tp"),
            P(("shard", "ctx"), "tp"),
            P(("shard", "ctx"), "tp"),
            P("tp", ("shard", "ctx")),
            P(("shard", "ctx"), "tp"),
            P(("shard", "ctx"), "tp"),
            P(("shard", "ctx"), "tp"),
            P("tp", ("shard", "ctx")),
            P(("shard", "ctx"), "tp"),
            P("tp", ("shard", "ctx")),
            P("tp"),
            P("tp"),
            P("tp"),
            P("tp"),
            P("tp"),
            P(),
            P(),
            P(),
            P(),
            P(),
            P(),
            P(),
            P(),
            P(),
        ),
        check_vma=False,
    )
```

```python
from functools import partial

import jax
import jax.numpy as jnp
from jax import lax
from jax.experimental import pallas as pl
from jax.experimental.pallas import tpu as pltpu
from jax.sharding import PartitionSpec as P

HDIM = 64
W = 1024
TILE = 256


EPSILON = 1e-05
NEGATIVE = -1e30
VMEM = 32 * 1024 * 1024


def matmul(left, right):
    return jnp.dot(left, right, preferred_element_type=jnp.float32)


def contract(form, left, right):
    return jnp.einsum(form, left, right, preferred_element_type=jnp.float32)


def low(value):
    return value.astype(jnp.bfloat16)


def wide(value):
    return value.astype(jnp.float32)


def swap(array, axis, bit):
    return lax.ppermute(array, axis, [(i, i ^ bit) for i in range(lax.axis_size(axis))])


def shift(array, axis, by):
    count = lax.axis_size(axis)
    pairs = [(i, i + by) for i in range(count) if 0 <= i + by < count]
    return lax.ppermute(array, axis, pairs)


def steps_of(*axes):
    steps = []
    for axis in axes:
        bit = lax.axis_size(axis) // 2
        while bit:
            steps.append((axis, bit))
            bit //= 2
    return steps


def after(value, *others):
    others = [other for other in others if other is not None]
    return lax.optimization_barrier((value, *others))[0] if others else value


def gather_tree(array, steps, start=None, used=None):
    for n, (axis, bit) in enumerate(steps):
        arrived = swap(after(array, start if n == 0 else None), axis, bit)
        array = jnp.concatenate([after(array, used if n == len(steps) - 1 else None), arrived])
    return array


def scatter_more(total, steps, start=None, used=None):
    for n, (axis, bit) in enumerate(reversed(steps)):
        half = total.shape[0] // 2
        arrived = swap(after(low(total[half:]), start if n == 0 else None), axis, bit)
        kept = after(total[:half], used if n == len(steps) - 1 else None)
        total = kept + wide(arrived)
    return total


def scatter_tree(make, size, steps, used=None, start=None):
    axis, bit = steps[-1]
    half = size // 2
    arrived = swap(after(low(make(slice(half, size))), start), axis, bit)
    total = after(make(slice(0, half)), used) + wide(arrived)
    return scatter_more(total, steps[:-1])


def all_sum(value, steps):
    for axis, bit in steps:
        value = value + swap(value, axis, bit)
    return value


def flat_bit(step, axes):
    axis, bit = step
    for other in axes[axes.index(axis) + 1 :]:
        bit = bit * lax.axis_size(other)
    return bit


def masks_of(axes, steps):
    masks = [0]
    for step in steps:
        masks = masks + [m | flat_bit(step, axes) for m in masks]
    return masks


def cross_over(blocks, axes):
    index = lax.axis_index(axes)
    bit = 1
    while bit < len(blocks):
        odd = (index & bit) != 0
        blocks = [jnp.where(odd, blocks[m ^ bit], blocks[m]) for m in range(len(blocks))]
        bit *= 2
    return blocks


def split(array, dim, count):
    size = array.shape[dim] // count
    return [lax.slice_in_dim(array, m * size, (m + 1) * size, axis=dim) for m in range(count)]


def to_tree(array, dim, axes, steps):
    masks = masks_of(axes, steps)
    blocks = cross_over(split(array, dim, len(masks)), axes)
    return jnp.concatenate([blocks[m] for m in masks], axis=dim)


def from_tree(array, dim, axes, steps):
    masks = masks_of(axes, steps)
    blocks = split(array, dim, len(masks))
    blocks = cross_over([blocks[masks.index(m)] for m in range(len(masks))], axes)
    return jnp.concatenate(blocks, axis=dim)


def in_tree(block, bits):
    return sum(((block >> k) & 1) << (bits - 1 - k) for k in range(bits))


def stack_heads(value, heads, turned):
    feature = lax.broadcasted_iota(jnp.int32, value.shape, 0 if turned else 1) // HDIM
    zero = jnp.zeros_like(value)
    parts = [jnp.where(feature == h, value, zero) for h in range(heads)]
    return jnp.concatenate(parts, axis=1 if turned else 0)


def allowed_in(lower, query, key_start, count):
    key = key_start + lax.broadcasted_iota(jnp.int32, (count, lower.shape[1]), 0)
    return (key >= lower) & (key <= query)


def along_heads(row, heads):
    return jnp.concatenate([row] * heads, axis=1)


def tile_of(ref, index, count, columns=None):
    rows = pl.ds(pl.multiple_of(index * count, count), count)
    return ref[rows, :] if columns is None else ref[rows, columns]


def lanes_of(index, count):
    return pl.ds(pl.multiple_of(index * count, count), count)


def attend_kernel(width, masked, *refs):
    if masked:
        meta, lower_ref, source_ref, old_ref, mixed_ref, mixed_t_ref, lse_ref, acc_ref = refs
        query_ref, first = source_ref, width
    else:
        query_ref, source_ref, mixed_ref, mixed_t_ref, lse_ref, acc_ref = refs
        first = 0
    heads, count = width // HDIM, TILE
    steps = mixed_ref.shape[0] // count
    bits = steps.bit_length() - 1

    @pl.loop(0, steps)
    def _(step):
        stacked = stack_heads(tile_of(query_ref, step, count, slice(0, width)).T, heads, True)
        acc_ref[...] = jnp.zeros_like(acc_ref)
        if masked:
            tile = in_tree(step, bits) ^ meta[0]
            lower = along_heads(lower_ref[:, lanes_of(step, count)], heads)
            place_of = tile * count + lax.broadcasted_iota(jnp.int32, (1, count), 1)
            place_of = along_heads(place_of, heads)

        def add(carry, ref, column, place, key_tile, masking, size=count):
            keys = tile_of(ref, place, size, slice(column, column + width))
            values_t = tile_of(ref, place, size, slice(column + width, column + 2 * width)).T
            top, total = carry
            scores = matmul(keys, stacked)
            if masking:
                ok = allowed_in(lower, place_of, key_tile * count, count)
                scores = jnp.where(ok, scores, NEGATIVE)
            higher = jnp.maximum(top, jnp.max(scores, axis=0, keepdims=True))
            expo = jnp.exp(scores - higher)
            scale = jnp.exp(top - higher)
            total = total * scale + jnp.sum(expo, axis=0, keepdims=True)
            expo = low(expo)
            for h in range(heads):
                part, lanes = slice(h * HDIM, (h + 1) * HDIM), slice(h * count, (h + 1) * count)
                acc_ref[part, :] = acc_ref[part, :] * scale[:, lanes] + matmul(
                    values_t[part, :], expo[:, lanes]
                )
            return higher, total

        carry = (
            jnp.full((1, heads * count), NEGATIVE, jnp.float32),
            jnp.zeros((1, heads * count), jnp.float32),
        )
        if masked:
            least = meta[1 + step]
            here = lambda n, c: add(
                c, source_ref, first, in_tree((tile - n) ^ meta[0], bits), tile - n, True
            )
            carry = lax.fori_loop(0, tile - jnp.maximum(least, 0) + 1, here, carry)
            before = lambda n, c: add(
                c, old_ref, 0, in_tree((n + steps) ^ meta[0], bits), n, True
            )
            carry = lax.fori_loop(least, 0, before, carry)
        else:
            every = lambda n, c: add(c, source_ref, first, n, n, False, 2 * count)
            carry = lax.fori_loop(0, source_ref.shape[0] // (2 * count), every, carry)
        top, total = carry
        lse = top + jnp.log(total)
        whole = lanes_of(step, count)
        for h in range(heads):
            part, lanes = slice(h * HDIM, (h + 1) * HDIM), slice(h * count, (h + 1) * count)
            acc_ref[part, :] = acc_ref[part, :] / total[:, lanes]
            lse_ref[h : h + 1, whole] = lse[:, lanes]
        mixed_t_ref[:, whole] = acc_ref[...]
        mixed_ref[whole, :] = low(acc_ref[...].T)


def attend_back_kernel(width, kind, *refs):
    refs = list(refs)
    masked, old = kind != "cross", kind == "old"
    if masked:
        meta, lower_ref = refs.pop(0), refs.pop(0)
    start_ref = refs.pop(0) if kind == "own" else None
    query_ref = refs.pop(0)
    grad_ref, mixed_t_ref, lse_ref = refs[:3]
    refs = refs[3:]
    source_ref = query_ref if kind == "own" else refs.pop(0)
    first = width if kind == "own" else 0
    grad_query_ref, grad_kv_ref, keys_acc, values_acc, query_acc = refs
    heads, count = width // HDIM, TILE
    steps = grad_ref.shape[0] // count
    bits = steps.bit_length() - 1
    keys_acc[...] = jnp.zeros_like(keys_acc)
    values_acc[...] = jnp.zeros_like(values_acc)

    def of_queries(step):
        whole = lanes_of(step, count)
        query = tile_of(query_ref, step, count, slice(0, width))
        grad = tile_of(grad_ref, step, count)
        grad_t = grad.T
        stacked = stack_heads(query, heads, False)
        stacked_t = stack_heads(query.T, heads, True)
        stacked_grad = stack_heads(grad, heads, False)
        stacked_grad_t = stack_heads(grad_t, heads, True)
        weighed = wide(grad_t) * mixed_t_ref[:, whole]
        lse = jnp.concatenate([lse_ref[h : h + 1, whole] for h in range(heads)], axis=1)
        inner = jnp.concatenate(
            [
                jnp.sum(weighed[h * HDIM : (h + 1) * HDIM, :], axis=0, keepdims=True)
                for h in range(heads)
            ],
            axis=1,
        )
        if masked:
            tile = in_tree(step, bits) ^ meta[0]
            lower = along_heads(lower_ref[:, whole], heads)
            place_of = tile * count + lax.broadcasted_iota(jnp.int32, (1, count), 1)
            place_of = along_heads(place_of, heads)

        def add(place, key_tile, size=count):
            rows = pl.ds(pl.multiple_of(place * size, size), size)
            keys = source_ref[rows, first : first + width]
            values = source_ref[rows, first + width : first + 2 * width]
            keys_t = keys.T
            probs = jnp.exp(matmul(keys, stacked_t) - lse)
            if masked:
                ok = allowed_in(lower, place_of, key_tile * count, count)
                probs = jnp.where(ok, probs, 0.0)
            slopes = low(probs * (matmul(values, stacked_grad_t) - inner))
            values_acc[rows, :] += matmul(low(probs), stacked_grad)
            keys_acc[rows, :] += matmul(slopes, stacked)
            for h in range(heads):
                part, lanes = slice(h * HDIM, (h + 1) * HDIM), slice(h * count, (h + 1) * count)
                query_acc[part, :] += matmul(keys_t[part, :], slopes[:, lanes])

        if not masked:
            pl.loop(0, source_ref.shape[0] // (2 * count))(lambda n: add(n, n, 2 * count))
        elif old:
            pl.loop(meta[1 + step], 0)(lambda n: add(in_tree((n + steps) ^ meta[0], bits), n))
        else:
            pl.loop(jnp.maximum(meta[1 + step], 0), tile + 1)(
                lambda n: add(in_tree(n ^ meta[0], bits), n)
            )

    @pl.loop(0, steps)
    def _(step):
        whole = lanes_of(step, count)
        if start_ref is None:
            query_acc[...] = jnp.zeros_like(query_acc)
        else:
            query_acc[...] = start_ref[:, whole]
        if old:
            pl.when(meta[1 + step] < 0)(lambda: of_queries(step))
            grad_query_ref[:, whole] = query_acc[...]
        else:
            of_queries(step)
            grad_query_ref[whole, :] = low(query_acc[...].T)

    grad_kv_ref[:, :width] = keys_acc[...].astype(grad_kv_ref.dtype)
    grad_kv_ref[:, width:] = values_acc[...].astype(grad_kv_ref.dtype)


IN_VMEM = pl.BlockSpec(memory_space=pltpu.VMEM)
IN_SMEM = pl.BlockSpec(memory_space=pltpu.SMEM)


def attend(width, query, source, meta=None, lower=None, old=None):
    rows = query.shape[0]
    heads = width // HDIM
    masked = old is not None
    inputs = [meta, lower, source, old] if masked else [query, source]
    specs = [IN_SMEM if masked else IN_VMEM] + [IN_VMEM] * (len(inputs) - 1)
    pairs = rows * source.shape[0] * width
    return pl.pallas_call(
        partial(attend_kernel, width, masked),
        in_specs=specs,
        out_specs=[IN_VMEM] * 3,
        out_shape=[
            jax.ShapeDtypeStruct((rows, width), jnp.bfloat16),
            jax.ShapeDtypeStruct((width, rows), jnp.float32),
            jax.ShapeDtypeStruct((heads, rows), jnp.float32),
        ],
        scratch_shapes=[pltpu.VMEM((width, TILE), jnp.float32)],
        compiler_params=pltpu.CompilerParams(vmem_limit_bytes=VMEM),
        cost_estimate=pl.CostEstimate(
            flops=48 * pairs, bytes_accessed=8 * rows * width, transcendentals=0
        ),
    )(*inputs)


def attend_back(width, kind, query, grad, mixed_t, lse, source=None, meta=None, lower=None, start=None):
    rows = grad.shape[0]
    inputs = [] if kind == "cross" else [meta, lower]
    inputs += [start] if kind == "own" else []
    inputs += [query, grad, mixed_t, lse] + ([] if kind == "own" else [source])
    specs = [IN_VMEM] * len(inputs)
    if kind != "cross":
        specs[0] = IN_SMEM
    count = (query if kind == "own" else source).shape[0]
    pairs = rows * count * width
    return pl.pallas_call(
        partial(attend_back_kernel, width, kind),
        in_specs=specs,
        out_specs=[IN_VMEM] * 2,
        out_shape=[
            jax.ShapeDtypeStruct((width, rows), jnp.float32)
            if kind == "old"
            else jax.ShapeDtypeStruct((rows, width), jnp.bfloat16),
            jax.ShapeDtypeStruct(
                (count, 2 * width), jnp.float32 if kind == "cross" else jnp.bfloat16
            ),
        ],
        scratch_shapes=[
            pltpu.VMEM((count, width), jnp.float32),
            pltpu.VMEM((count, width), jnp.float32),
            pltpu.VMEM((width, TILE), jnp.float32),
        ],
        compiler_params=pltpu.CompilerParams(vmem_limit_bytes=VMEM),
        cost_estimate=pl.CostEstimate(
            flops=64 * pairs, bytes_accessed=16 * rows * width, transcendentals=0
        ),
    )(*inputs)


def layer_norm(value, gain, shift_by):
    centre = value - jnp.mean(value, axis=-1, keepdims=True)
    rstd = lax.rsqrt(jnp.mean(centre * centre, axis=-1, keepdims=True) + EPSILON)
    normed = centre * rstd
    return (normed * gain + shift_by, normed, rstd)


def norm_back(grad_out, normed, rstd, gain):
    scaled = grad_out * gain
    inner = scaled - jnp.mean(scaled, axis=-1, keepdims=True)
    inner = inner - normed * jnp.mean(scaled * normed, axis=-1, keepdims=True)
    return (rstd * inner, jnp.sum(grad_out * normed, axis=0), jnp.sum(grad_out, axis=0))


def gelu_and_slope(value):
    phi = 0.5 * (1.0 + lax.erf(value * 0.7071067811865476))
    bell = jnp.exp(-0.5 * value * value) * 0.3989422804014327
    return value * phi, phi + value * bell


def column_sum(value):
    return jnp.sum(wide(value), axis=0)


def per_device(
    inputs,
    encoded,
    doc_lengths,
    cotangent,
    query_weight,
    key_weight,
    value_weight,
    out_weight,
    memory_query,
    memory_key,
    memory_value,
    memory_out,
    up_weight,
    down_weight,
    query_bias,
    value_bias,
    memory_qbias,
    memory_vbias,
    up_bias,
    out_bias,
    memory_obias,
    down_bias,
    gain_self,
    shift_self,
    gain_memory,
    shift_memory,
    gain_dense,
    shift_dense,
):
    tp_index = lax.axis_index("tp")
    share_rows = inputs.shape[1]
    rows = share_rows * lax.axis_size("tp")
    width = query_weight.shape[1]
    base = lax.axis_index("ctx") * rows
    row_steps = steps_of("tp")
    weight_steps = steps_of("shard", "ctx")
    features = ("shard", "ctx")

    def turned(array, dim):
        return to_tree(array, dim, features, weight_steps)

    def turned_back(array, dim):
        return from_tree(array, dim, features, weight_steps)

    def gather_rows(piece):
        return gather_tree(piece, row_steps)

    def scatter_rows(make):
        return scatter_tree(make, rows, row_steps)

    def own_half(weight):
        part = weight.shape[0] // lax.axis_size("ctx")
        return lax.dynamic_slice_in_dim(weight, lax.axis_index("ctx") * part, part, 0)

    ctx_steps = steps_of("ctx")
    far_steps, near_steps = steps_of("shard")[:-1], steps_of("shard")[-1:]
    share = turned(inputs[0], 1)
    old_share = turned(shift(inputs[0], "ctx", 1), 1)
    inputs_rows = lax.optimization_barrier(gather_rows(share))
    old_rows = lax.optimization_barrier(gather_rows(old_share))
    qkv_own = own_half(jnp.concatenate([query_weight, key_weight, value_weight], axis=1))
    qkv_far = gather_tree(qkv_own, far_steps)
    qkv_near = gather_tree(qkv_far, near_steps)
    qkv_full = gather_tree(qkv_near, ctx_steps)
    out_far = gather_tree(own_half(out_weight.T), far_steps, qkv_far)
    out_near = gather_tree(out_far, near_steps, qkv_near)
    small_own = jnp.concatenate([memory_key, memory_value, memory_query, memory_out.T], axis=1)
    small_far = gather_tree(own_half(small_own), far_steps, qkv_near)
    up_own = own_half(up_weight)
    down_own = own_half(down_weight.T)
    states = to_tree(turned(encoded[0], 1), 0, ("tp",), row_steps)
    vectors = turned(
        jnp.stack(
            [
                out_bias,
                memory_obias,
                down_bias,
                gain_self,
                shift_self,
                gain_memory,
                shift_memory,
                gain_dense,
                shift_dense,
            ]
        ),
        1,
    )
    (
        out_bias,
        memory_obias,
        down_bias,
        gain_self,
        shift_self,
        gain_memory,
        shift_memory,
        gain_dense,
        shift_dense,
    ) = [vectors[i] for i in range(9)]
    upstream = wide(turned(cotangent[0], 1))

    ends = jnp.cumsum(doc_lengths[0], dtype=jnp.int32)
    masks = jnp.asarray(masks_of(("tp",), row_steps), jnp.int32)
    starts = (masks ^ tp_index) * share_rows
    place = base + (starts[:, None] + jnp.arange(share_rows, dtype=jnp.int32)).reshape(-1)
    opens = jnp.max(jnp.where(place[:, None] >= ends[None, :], ends[None, :], 0), axis=1)
    lower = jnp.maximum(opens, place - (W - 1)) - base
    least = lower.reshape(-1, TILE)[:, 0] // TILE
    meta = jnp.concatenate([tp_index[None].astype(jnp.int32), least])
    lower = lower[None, :]

    zeros = jnp.zeros_like(query_bias)
    qkv = low(
        (matmul(inputs_rows, qkv_full) + jnp.concatenate([query_bias, zeros, value_bias]))
        * jnp.concatenate([zeros + 0.125, zeros + 1.0, zeros + 1.0])
    )
    old_kv = low(matmul(old_rows, qkv_full[:, width:]) + jnp.concatenate([zeros, value_bias]))
    small_near = gather_tree(small_far, near_steps, None, qkv)
    qkv = after(qkv, out_near, small_near)
    mixed, mixed_t, self_lse = attend(width, qkv, qkv, meta, lower, old_kv)
    out_full = gather_tree(out_near, ctx_steps, qkv_full, mixed)
    mkv_full = gather_tree(small_near[:, : 2 * width], ctx_steps, None, mixed)
    up_far = gather_tree(up_own, far_steps, small_near, mixed)
    mixed = after(mixed, mkv_full, up_far)
    attn_part = scatter_tree(
        lambda s: contract("rk,dk->rd", mixed[s], out_full), rows, row_steps[-1:]
    )

    mkv_own = low(
        matmul(states, after(mkv_full, attn_part)) + jnp.concatenate([zeros, memory_vbias])
    )

    def weight_terms(*pairs):
        def make(s):
            return jnp.concatenate(
                [contract("rd,rk->dk", left[:, s], right) for left, right in pairs], axis=1
            )

        return make

    model = share.shape[1]

    attn_share = scatter_more(attn_part, row_steps[:-1])
    first, normed_one, rstd_one = layer_norm(
        wide(share) + attn_share + out_bias, gain_self, shift_self
    )
    up_near = gather_tree(up_far, near_steps, mixed, attn_part)
    down_far = gather_tree(down_own, far_steps, mixed, attn_part)
    mkv = gather_tree(mkv_own, ctx_steps)
    small_full = gather_tree(small_near[:, 2 * width :], ctx_steps, mixed, attn_part)
    first_low = after(low(first), up_near, down_far, mkv, small_full)
    mquery_full, mout_full = small_full[:, :width], small_full[:, width:]
    half_rows = gather_tree(first_low, row_steps[:-1])
    down_near = gather_tree(down_far, near_steps, first_low, half_rows)
    up_ready = gather_tree(split(up_near, 1, 2)[0], ctx_steps, first_low, half_rows)
    half_rows = after(half_rows, down_near, up_ready)
    first_rows = gather_tree(half_rows, row_steps[-1:])
    mquery = low((matmul(first_rows, mquery_full) + memory_qbias) * 0.125)
    cross_mixed, cross_mixed_t, cross_lse = attend(width, mquery, mkv)
    up_parts = [
        up_ready,
        gather_tree(split(up_near, 1, 2)[1], ctx_steps, half_rows, cross_mixed),
    ]
    cross_mixed = after(cross_mixed, up_parts[1])
    cross_part = scatter_tree(
        lambda s: contract("rk,dk->rd", cross_mixed[s], mout_full), rows, row_steps[-1:]
    )
    cross_share = scatter_more(cross_part, row_steps[:-1])
    second, normed_two, rstd_two = layer_norm(
        first + cross_share + memory_obias, gain_memory, shift_memory
    )
    down_ready = gather_tree(split(down_near, 1, 2)[0], ctx_steps, cross_mixed, cross_part)
    second_low = after(low(second), down_ready)
    half_second = gather_tree(second_low, row_steps[:-1])
    down_parts = [
        down_ready,
        gather_tree(split(down_near, 1, 2)[1], ctx_steps, second_low, half_second),
    ]
    second_rows = gather_tree(after(half_second, down_parts[1]), row_steps[-1:])
    up_full = lax.optimization_barrier(
        jnp.concatenate([after(up_parts[0], cross_part), up_parts[1]], axis=1)
    )
    act, slope = gelu_and_slope(matmul(second_rows, up_full) + up_bias)
    act_low, slope_low = low(act), low(slope)

    def dense_term(s):
        terms = [
            contract("rf,df->rd", a, part)
            for a, part in zip(split(act_low[s], 1, 2), down_parts, strict=True)
        ]
        return terms[0] + terms[1]

    dense_part = scatter_tree(dense_term, rows, row_steps[-1:])
    dense_share = scatter_more(dense_part, row_steps[:-1])
    down_full = lax.optimization_barrier(
        jnp.concatenate([after(down_parts[0], dense_part), down_parts[1]], axis=1)
    )
    result, normed_three, rstd_three = layer_norm(
        second + dense_share + down_bias, gain_dense, shift_dense
    )
    grad_three, gain_dense_grad, shift_dense_grad = norm_back(
        upstream, normed_three, rstd_three, gain_dense
    )
    dense_low = low(grad_three)
    dense_rows = gather_rows(dense_low)
    hidden_low = low(matmul(dense_rows, down_full) * wide(slope_low))
    second_share = scatter_rows(lambda s: contract("rf,df->rd", hidden_low[s], up_full))
    grad_two, gain_memory_grad, shift_memory_grad = norm_back(
        grad_three + second_share, normed_two, rstd_two, gain_memory
    )

    cross_low = low(grad_two)
    cross_rows = gather_rows(cross_low)
    down_part = scatter_tree(weight_terms((dense_rows, act_low)), model, ctx_steps, cross_rows)
    grad_cross_mixed = low(matmul(cross_rows, mout_full))
    mquery_back, mkv_sum = attend_back(
        width, "cross", mquery, grad_cross_mixed, cross_mixed_t, cross_lse, mkv
    )
    mquery_pre = mquery_back * 0.125
    down_near_grad = scatter_more(down_part, near_steps, None, mquery_pre)
    up_part = scatter_tree(
        weight_terms((second_rows, hidden_low)), model, ctx_steps, mquery_pre, cross_low
    )
    first_part = scatter_tree(
        lambda s: contract("rk,dk->rd", mquery_pre[s], mquery_full), rows, row_steps[-1:]
    )
    first_share = scatter_more(first_part, row_steps[:-1])
    grad_one, gain_self_grad, shift_self_grad = norm_back(
        grad_two + first_share, normed_one, rstd_one, gain_self
    )
    self_low = low(grad_one)
    self_rows = gather_rows(self_low)
    down_grads = scatter_more(down_near_grad, far_steps, first_part, self_low)
    up_near_grad = scatter_more(up_part, near_steps, first_part, self_low)
    up_grads = scatter_more(up_near_grad, far_steps, None, self_rows)
    mkv_back = after(mkv_sum, first_part)
    mkv_low = low(scatter_tree(lambda s: mkv_back[s], mkv_back.shape[0], ctx_steps))
    encoded_grad = scatter_tree(
        lambda s: contract("ek,dk->ed", mkv_low[s], mkv_full), states.shape[0], row_steps
    )
    small_part = scatter_tree(
        weight_terms((states, mkv_low), (first_rows, mquery_pre), (cross_rows, cross_mixed)),
        model,
        ctx_steps,
        self_rows,
    )
    grad_self = after(low(matmul(self_rows, out_full)), small_part)

    query_start, old_back = attend_back(
        width, "old", qkv, grad_self, mixed_t, self_lse, old_kv, meta, lower
    )
    back = shift(old_back, "ctx", -1)
    small_near_grads = scatter_more(small_part, near_steps, None, old_back)
    grad_self_later = after(grad_self, small_near_grads, query_start)
    query_back, kv_back = attend_back(
        width, "own", qkv, grad_self_later, mixed_t, self_lse, None, meta, lower, query_start
    )
    query_pre = query_back * 0.125
    small_grads = scatter_more(small_near_grads, far_steps, None, query_pre)
    own_back = jnp.concatenate([query_pre, kv_back], axis=1)

    def qkv_terms(s):
        own = contract("rd,rk->dk", inputs_rows[:, s], own_back)
        old = contract("rd,rk->dk", old_rows[:, s], old_back)
        return own + jnp.pad(old, ((0, 0), (width, 0)))

    kv_all = low(wide(kv_back) + wide(back))

    def inputs_term(s):
        term = contract("rk,dk->rd", query_pre[s], qkv_full[:, :width])
        return term + contract("rk,dk->rd", kv_all[s], qkv_full[:, width:])

    inputs_part = scatter_tree(inputs_term, rows, row_steps[-1:])
    inputs_grad = grad_one + scatter_more(inputs_part, row_steps[:-1])
    sent = low(inputs_part[inputs_part.shape[0] // 2 :])
    qkv_grads = scatter_more(
        scatter_tree(qkv_terms, model, ctx_steps, sent), weight_steps[: -len(ctx_steps)]
    )
    out_part = scatter_tree(weight_terms((self_rows, mixed)), model, ctx_steps, sent)
    out_grads = scatter_more(out_part, steps_of("shard"))

    everywhere = jnp.stack(
        [
            column_sum(self_low),
            column_sum(cross_low),
            column_sum(dense_low),
            gain_self_grad,
            shift_self_grad,
            gain_memory_grad,
            shift_memory_grad,
            gain_dense_grad,
            shift_dense_grad,
        ]
    )
    everywhere = all_sum(turned_back(everywhere, 1), row_steps)
    by_heads = jnp.concatenate(
        [
            column_sum(query_pre),
            column_sum(kv_back[:, width:]) + column_sum(old_back[:, width:]),
            column_sum(mquery_pre),
            column_sum(mkv_low[:, width:]),
            column_sum(hidden_low),
        ]
    )
    lanes = 128
    sums = all_sum(
        after(
            jnp.concatenate([everywhere.reshape(-1, lanes), by_heads.reshape(-1, lanes)], axis=0),
            sent,
        ),
        weight_steps,
    )
    cut = everywhere.size // lanes
    totals = sums[:cut].reshape(everywhere.shape)
    head_totals = sums[cut:].reshape(-1)
    return (
        turned_back(low(result), 1)[None],
        turned_back(inputs_grad, 1)[None],
        turned_back(encoded_grad, 1)[None],
        qkv_grads[:, :width],
        qkv_grads[:, width : 2 * width],
        qkv_grads[:, 2 * width :],
        out_grads.T,
        small_grads[:, 2 * width : 3 * width],
        small_grads[:, :width],
        small_grads[:, width : 2 * width],
        small_grads[:, 3 * width :].T,
        up_grads,
        down_grads.T,
        head_totals[:width],
        head_totals[width : 2 * width],
        head_totals[2 * width : 3 * width],
        head_totals[3 * width : 4 * width],
        head_totals[4 * width :],
        totals[0],
        totals[1],
        totals[2],
        totals[3],
        totals[4],
        totals[5],
        totals[6],
        totals[7],
        totals[8],
    )


def solution(mesh):
    placed = (
        P("shard", ("ctx", "tp"), None),
        P("shard", "ctx", None),
        P("shard", None),
        P("shard", ("ctx", "tp"), None),
        P("shard", "tp"),
        P("shard", "tp"),
        P("shard", "tp"),
        P("tp", "shard"),
        P("shard", "tp"),
        P("shard", "tp"),
        P("shard", "tp"),
        P("tp", "shard"),
        P("shard", "tp"),
        P("tp", "shard"),
        P("tp"),
        P("tp"),
        P("tp"),
        P("tp"),
        P("tp"),
        P(),
        P(),
        P(),
        P(),
        P(),
        P(),
        P(),
        P(),
        P(),
    )
    return jax.shard_map(
        per_device,
        mesh=mesh,
        in_specs=placed,
        out_specs=(
            P("shard", ("ctx", "tp"), None),
            P("shard", ("ctx", "tp"), None),
            P("shard", ("ctx", "tp"), None),
            P(("shard", "ctx"), "tp"),
            P(("shard", "ctx"), "tp"),
            P(("shard", "ctx"), "tp"),
            P("tp", ("shard", "ctx")),
            P(("shard", "ctx"), "tp"),
            P(("shard", "ctx"), "tp"),
            P(("shard", "ctx"), "tp"),
            P("tp", ("shard", "ctx")),
            P(("shard", "ctx"), "tp"),
            P("tp", ("shard", "ctx")),
            P("tp"),
            P("tp"),
            P("tp"),
            P("tp"),
            P("tp"),
            P(),
            P(),
            P(),
            P(),
            P(),
            P(),
            P(),
            P(),
            P(),
        ),
        check_vma=False,
    )
```

```python
from functools import partial

import jax
import jax.numpy as jnp
from jax import lax
from jax.experimental import pallas as pl
from jax.experimental.layout import Layout, with_layout_constraint
from jax.experimental.pallas import tpu as pltpu
from jax.sharding import PartitionSpec as P

HDIM = 64
W = 1024
TILE = 256


EPSILON = 1e-05
NEGATIVE = -1e30
VMEM = 32 * 1024 * 1024


def matmul(left, right):
    return jnp.dot(left, right, preferred_element_type=jnp.float32)


def contract(form, left, right):
    return jnp.einsum(form, left, right, preferred_element_type=jnp.float32)


def low(value):
    return value.astype(jnp.bfloat16)


def wide(value):
    return value.astype(jnp.float32)


def swap(array, axis, bit):
    return lax.ppermute(array, axis, [(i, i ^ bit) for i in range(lax.axis_size(axis))])


def shift(array, axis, by):
    count = lax.axis_size(axis)
    pairs = [(i, i + by) for i in range(count) if 0 <= i + by < count]
    return lax.ppermute(array, axis, pairs)


def steps_of(*axes):
    steps = []
    for axis in axes:
        bit = lax.axis_size(axis) // 2
        while bit:
            steps.append((axis, bit))
            bit //= 2
    return steps


def after(value, *others):
    others = [other for other in others if other is not None]
    return lax.optimization_barrier((value, *others))[0] if others else value


def gather_tree(array, steps, start=None, used=None):
    for n, (axis, bit) in enumerate(steps):
        arrived = swap(after(array, start if n == 0 else None), axis, bit)
        array = jnp.concatenate([after(array, used if n == len(steps) - 1 else None), arrived])
    return array


def scatter_more(total, steps, start=None, used=None):
    for n, (axis, bit) in enumerate(reversed(steps)):
        half = total.shape[0] // 2
        arrived = swap(after(low(total[half:]), start if n == 0 else None), axis, bit)
        kept = after(total[:half], used if n == len(steps) - 1 else None)
        total = kept + wide(arrived)
    return total


def scatter_tree(make, size, steps, used=None, start=None, far=None):
    axis, bit = steps[-1]
    half = size // 2
    if far is None:
        far = low(make(slice(half, size)))
    arrived = swap(after(far, start), axis, bit)
    total = after(make(slice(0, half)), used) + wide(arrived)
    return scatter_more(total, steps[:-1])


def all_sum(value, steps):
    for axis, bit in steps:
        value = value + swap(value, axis, bit)
    return value


def flat_bit(step, axes):
    axis, bit = step
    for other in axes[axes.index(axis) + 1 :]:
        bit = bit * lax.axis_size(other)
    return bit


def masks_of(axes, steps):
    masks = [0]
    for step in steps:
        masks = masks + [m | flat_bit(step, axes) for m in masks]
    return masks


def cross_over(blocks, axes):
    index = lax.axis_index(axes)
    bit = 1
    while bit < len(blocks):
        odd = (index & bit) != 0
        blocks = [jnp.where(odd, blocks[m ^ bit], blocks[m]) for m in range(len(blocks))]
        bit *= 2
    return blocks


def split(array, dim, count):
    size = array.shape[dim] // count
    return [lax.slice_in_dim(array, m * size, (m + 1) * size, axis=dim) for m in range(count)]


def to_tree(array, dim, axes, steps):
    masks = masks_of(axes, steps)
    blocks = cross_over(split(array, dim, len(masks)), axes)
    return jnp.concatenate([blocks[m] for m in masks], axis=dim)


def from_tree(array, dim, axes, steps):
    masks = masks_of(axes, steps)
    blocks = split(array, dim, len(masks))
    blocks = cross_over([blocks[masks.index(m)] for m in range(len(masks))], axes)
    return jnp.concatenate(blocks, axis=dim)


def in_tree(block, bits):
    return sum(((block >> k) & 1) << (bits - 1 - k) for k in range(bits))


def stack_heads(value, heads, turned):
    feature = lax.broadcasted_iota(jnp.int32, value.shape, 0 if turned else 1) // HDIM
    zero = jnp.zeros_like(value)
    parts = [jnp.where(feature == h, value, zero) for h in range(heads)]
    return jnp.concatenate(parts, axis=1 if turned else 0)


def allowed_in(lower, query, key_start, count):
    key = key_start + lax.broadcasted_iota(jnp.int32, (count, lower.shape[1]), 0)
    return (key >= lower) & (key <= query)


def along_heads(row, heads):
    return jnp.concatenate([row] * heads, axis=1)


def tile_of(ref, index, count, columns=None):
    rows = pl.ds(pl.multiple_of(index * count, count), count)
    return ref[rows, :] if columns is None else ref[rows, columns]


def lanes_of(index, count):
    return pl.ds(pl.multiple_of(index * count, count), count)


def attend_kernel(width, masked, *refs):
    if masked:
        meta, lower_ref, source_ref, old_ref, mixed_ref, mixed_t_ref, lse_ref, acc_ref = refs
        query_ref, first = source_ref, width
    else:
        query_ref, source_ref, mixed_ref, mixed_t_ref, lse_ref, acc_ref = refs
        first = 0
    heads, count = width // HDIM, TILE
    steps = mixed_ref.shape[0] // count
    bits = steps.bit_length() - 1

    @pl.loop(0, steps)
    def _(step):
        stacked = stack_heads(tile_of(query_ref, step, count, slice(0, width)).T, heads, True)
        acc_ref[...] = jnp.zeros_like(acc_ref)
        if masked:
            tile = in_tree(step, bits) ^ meta[0]
            lower = along_heads(lower_ref[:, lanes_of(step, count)], heads)
            place_of = tile * count + lax.broadcasted_iota(jnp.int32, (1, count), 1)
            place_of = along_heads(place_of, heads)

        def add(carry, ref, column, place, key_tile, masking, size=count):
            keys = tile_of(ref, place, size, slice(column, column + width))
            values_t = tile_of(ref, place, size, slice(column + width, column + 2 * width)).T
            top, total = carry
            scores = matmul(keys, stacked)
            if masking:
                ok = allowed_in(lower, place_of, key_tile * count, count)
                scores = jnp.where(ok, scores, NEGATIVE)
            higher = jnp.maximum(top, jnp.max(scores, axis=0, keepdims=True))
            expo = jnp.exp(scores - higher)
            scale = jnp.exp(top - higher)
            total = total * scale + jnp.sum(expo, axis=0, keepdims=True)
            expo = low(expo)
            for h in range(heads):
                part, lanes = slice(h * HDIM, (h + 1) * HDIM), slice(h * count, (h + 1) * count)
                acc_ref[part, :] = acc_ref[part, :] * scale[:, lanes] + matmul(
                    values_t[part, :], expo[:, lanes]
                )
            return higher, total

        carry = (
            jnp.full((1, heads * count), NEGATIVE, jnp.float32),
            jnp.zeros((1, heads * count), jnp.float32),
        )
        if masked:
            least = meta[1 + step]
            here = lambda n, c: add(
                c, source_ref, first, in_tree((tile - n) ^ meta[0], bits), tile - n, True
            )
            carry = lax.fori_loop(0, tile - jnp.maximum(least, 0) + 1, here, carry)
            before = lambda n, c: add(
                c, old_ref, 0, in_tree((n + steps) ^ meta[0], bits), n, True
            )
            carry = lax.fori_loop(least, 0, before, carry)
        else:
            every = lambda n, c: add(c, source_ref, first, n, n, False, 2 * count)
            carry = lax.fori_loop(0, source_ref.shape[0] // (2 * count), every, carry)
        top, total = carry
        lse = top + jnp.log(total)
        whole = lanes_of(step, count)
        for h in range(heads):
            part, lanes = slice(h * HDIM, (h + 1) * HDIM), slice(h * count, (h + 1) * count)
            acc_ref[part, :] = acc_ref[part, :] / total[:, lanes]
            lse_ref[h : h + 1, whole] = lse[:, lanes]
        mixed_t_ref[:, whole] = acc_ref[...]
        mixed_ref[whole, :] = low(acc_ref[...].T)


def attend_back_kernel(width, kind, *refs):
    refs = list(refs)
    masked, old = kind != "cross", kind == "old"
    if masked:
        meta, lower_ref = refs.pop(0), refs.pop(0)
    start_ref = refs.pop(0) if kind == "own" else None
    query_ref = refs.pop(0)
    grad_ref, mixed_t_ref, lse_ref = refs[:3]
    refs = refs[3:]
    source_ref = query_ref if kind == "own" else refs.pop(0)
    first = width if kind == "own" else 0
    grad_query_ref, grad_kv_ref, keys_acc, values_acc, query_acc = refs
    heads, count = width // HDIM, TILE
    steps = grad_ref.shape[0] // count
    bits = steps.bit_length() - 1
    keys_acc[...] = jnp.zeros_like(keys_acc)
    values_acc[...] = jnp.zeros_like(values_acc)

    def of_queries(step):
        whole = lanes_of(step, count)
        query = tile_of(query_ref, step, count, slice(0, width))
        grad = tile_of(grad_ref, step, count)
        grad_t = grad.T
        stacked = stack_heads(query, heads, False)
        stacked_t = stack_heads(query.T, heads, True)
        stacked_grad = stack_heads(grad, heads, False)
        stacked_grad_t = stack_heads(grad_t, heads, True)
        weighed = wide(grad_t) * mixed_t_ref[:, whole]
        lse = jnp.concatenate([lse_ref[h : h + 1, whole] for h in range(heads)], axis=1)
        inner = jnp.concatenate(
            [
                jnp.sum(weighed[h * HDIM : (h + 1) * HDIM, :], axis=0, keepdims=True)
                for h in range(heads)
            ],
            axis=1,
        )
        if masked:
            tile = in_tree(step, bits) ^ meta[0]
            lower = along_heads(lower_ref[:, whole], heads)
            place_of = tile * count + lax.broadcasted_iota(jnp.int32, (1, count), 1)
            place_of = along_heads(place_of, heads)

        def add(place, key_tile, size=count):
            rows = pl.ds(pl.multiple_of(place * size, size), size)
            keys = source_ref[rows, first : first + width]
            values = source_ref[rows, first + width : first + 2 * width]
            keys_t = keys.T
            probs = jnp.exp(matmul(keys, stacked_t) - lse)
            if masked:
                ok = allowed_in(lower, place_of, key_tile * count, count)
                probs = jnp.where(ok, probs, 0.0)
            slopes = low(probs * (matmul(values, stacked_grad_t) - inner))
            values_acc[rows, :] += matmul(low(probs), stacked_grad)
            keys_acc[rows, :] += matmul(slopes, stacked)
            for h in range(heads):
                part, lanes = slice(h * HDIM, (h + 1) * HDIM), slice(h * count, (h + 1) * count)
                query_acc[part, :] += matmul(keys_t[part, :], slopes[:, lanes])

        if not masked:
            pl.loop(0, source_ref.shape[0] // (2 * count))(lambda n: add(n, n, 2 * count))
        elif old:
            pl.loop(meta[1 + step], 0)(lambda n: add(in_tree((n + steps) ^ meta[0], bits), n))
        else:
            pl.loop(jnp.maximum(meta[1 + step], 0), tile + 1)(
                lambda n: add(in_tree(n ^ meta[0], bits), n)
            )

    @pl.loop(0, steps)
    def _(step):
        whole = lanes_of(step, count)
        if start_ref is None:
            query_acc[...] = jnp.zeros_like(query_acc)
        else:
            query_acc[...] = start_ref[:, whole]
        if old:
            pl.when(meta[1 + step] < 0)(lambda: of_queries(step))
            grad_query_ref[:, whole] = query_acc[...]
        else:
            of_queries(step)
            grad_query_ref[whole, :] = low(query_acc[...].T)

    grad_kv_ref[:, :width] = keys_acc[...].astype(grad_kv_ref.dtype)
    grad_kv_ref[:, width:] = values_acc[...].astype(grad_kv_ref.dtype)


IN_VMEM = pl.BlockSpec(memory_space=pltpu.VMEM)
IN_SMEM = pl.BlockSpec(memory_space=pltpu.SMEM)


def attend(width, query, source, meta=None, lower=None, old=None):
    rows = query.shape[0]
    heads = width // HDIM
    masked = old is not None
    inputs = [meta, lower, source, old] if masked else [query, source]
    specs = [IN_SMEM if masked else IN_VMEM] + [IN_VMEM] * (len(inputs) - 1)
    pairs = rows * source.shape[0] * width
    return pl.pallas_call(
        partial(attend_kernel, width, masked),
        in_specs=specs,
        out_specs=[IN_VMEM] * 3,
        out_shape=[
            jax.ShapeDtypeStruct((rows, width), jnp.bfloat16),
            jax.ShapeDtypeStruct((width, rows), jnp.float32),
            jax.ShapeDtypeStruct((heads, rows), jnp.float32),
        ],
        scratch_shapes=[pltpu.VMEM((width, TILE), jnp.float32)],
        compiler_params=pltpu.CompilerParams(vmem_limit_bytes=VMEM),
        cost_estimate=pl.CostEstimate(
            flops=48 * pairs, bytes_accessed=8 * rows * width, transcendentals=0
        ),
    )(*inputs)


def attend_back(width, kind, query, grad, mixed_t, lse, source=None, meta=None, lower=None, start=None):
    rows = grad.shape[0]
    inputs = [] if kind == "cross" else [meta, lower]
    inputs += [start] if kind == "own" else []
    inputs += [query, grad, mixed_t, lse] + ([] if kind == "own" else [source])
    specs = [IN_VMEM] * len(inputs)
    if kind != "cross":
        specs[0] = IN_SMEM
    count = (query if kind == "own" else source).shape[0]
    pairs = rows * count * width
    return pl.pallas_call(
        partial(attend_back_kernel, width, kind),
        in_specs=specs,
        out_specs=[IN_VMEM] * 2,
        out_shape=[
            jax.ShapeDtypeStruct((width, rows), jnp.float32)
            if kind == "old"
            else jax.ShapeDtypeStruct((rows, width), jnp.bfloat16),
            jax.ShapeDtypeStruct(
                (count, 2 * width), jnp.float32 if kind == "cross" else jnp.bfloat16
            ),
        ],
        scratch_shapes=[
            pltpu.VMEM((count, width), jnp.float32),
            pltpu.VMEM((count, width), jnp.float32),
            pltpu.VMEM((width, TILE), jnp.float32),
        ],
        compiler_params=pltpu.CompilerParams(vmem_limit_bytes=VMEM),
        cost_estimate=pl.CostEstimate(
            flops=64 * pairs, bytes_accessed=16 * rows * width, transcendentals=0
        ),
    )(*inputs)


def layer_norm(value, gain, shift_by):
    centre = value - jnp.mean(value, axis=-1, keepdims=True)
    rstd = lax.rsqrt(jnp.mean(centre * centre, axis=-1, keepdims=True) + EPSILON)
    normed = centre * rstd
    return (normed * gain + shift_by, normed, rstd)


def norm_back(grad_out, normed, rstd, gain):
    scaled = grad_out * gain
    inner = scaled - jnp.mean(scaled, axis=-1, keepdims=True)
    inner = inner - normed * jnp.mean(scaled * normed, axis=-1, keepdims=True)
    return (rstd * inner, jnp.sum(grad_out * normed, axis=0), jnp.sum(grad_out, axis=0))


def gelu_and_slope(value):
    phi = 0.5 * (1.0 + lax.erf(value * 0.7071067811865476))
    bell = jnp.exp(-0.5 * value * value) * 0.3989422804014327
    return value * phi, phi + value * bell


def column_sum(value):
    return jnp.sum(wide(value), axis=0)


def per_device(
    inputs,
    encoded,
    doc_lengths,
    cotangent,
    query_weight,
    key_weight,
    value_weight,
    out_weight,
    memory_query,
    memory_key,
    memory_value,
    memory_out,
    up_weight,
    down_weight,
    query_bias,
    value_bias,
    memory_qbias,
    memory_vbias,
    up_bias,
    out_bias,
    memory_obias,
    down_bias,
    gain_self,
    shift_self,
    gain_memory,
    shift_memory,
    gain_dense,
    shift_dense,
):
    tp_index = lax.axis_index("tp")
    share_rows = inputs.shape[1]
    rows = share_rows * lax.axis_size("tp")
    width = query_weight.shape[1]
    base = lax.axis_index("ctx") * rows
    row_steps = steps_of("tp")
    weight_steps = steps_of("shard", "ctx")
    features = ("shard", "ctx")

    def turned(array, dim):
        return to_tree(array, dim, features, weight_steps)

    def turned_back(array, dim):
        return from_tree(array, dim, features, weight_steps)

    def gather_rows(piece):
        return gather_tree(piece, row_steps)

    def scatter_rows(make):
        return scatter_tree(make, rows, row_steps)

    def own_half(weight):
        part = weight.shape[0] // lax.axis_size("ctx")
        return lax.dynamic_slice_in_dim(weight, lax.axis_index("ctx") * part, part, 0)

    ctx_steps = steps_of("ctx")
    far_steps, near_steps = steps_of("shard")[:-1], steps_of("shard")[-1:]
    share = turned(inputs[0], 1)
    old_share = turned(shift(inputs[0], "ctx", 1), 1)
    inputs_rows = lax.optimization_barrier(gather_rows(share))
    old_rows = lax.optimization_barrier(gather_rows(old_share))
    qkv_own = own_half(jnp.concatenate([query_weight, key_weight, value_weight], axis=1))
    qkv_far = gather_tree(qkv_own, far_steps)
    qkv_near = gather_tree(qkv_far, near_steps)
    qkv_full = gather_tree(qkv_near, ctx_steps)
    out_far = gather_tree(own_half(out_weight.T), far_steps, qkv_far)
    out_near = gather_tree(out_far, near_steps, qkv_near)
    small_own = jnp.concatenate([memory_key, memory_value, memory_query, memory_out.T], axis=1)
    small_own = with_layout_constraint(small_own, Layout((0, 1)))
    small_far = gather_tree(own_half(small_own), far_steps, qkv_near)
    up_own = own_half(up_weight)
    down_own = own_half(down_weight.T)
    states = to_tree(turned(encoded[0], 1), 0, ("tp",), row_steps)
    vectors = turned(
        jnp.stack(
            [
                out_bias,
                memory_obias,
                down_bias,
                gain_self,
                shift_self,
                gain_memory,
                shift_memory,
                gain_dense,
                shift_dense,
            ]
        ),
        1,
    )
    (
        out_bias,
        memory_obias,
        down_bias,
        gain_self,
        shift_self,
        gain_memory,
        shift_memory,
        gain_dense,
        shift_dense,
    ) = [vectors[i] for i in range(9)]
    upstream = wide(turned(cotangent[0], 1))

    ends = jnp.cumsum(doc_lengths[0], dtype=jnp.int32)
    masks = jnp.asarray(masks_of(("tp",), row_steps), jnp.int32)
    starts = (masks ^ tp_index) * share_rows
    place = base + (starts[:, None] + jnp.arange(share_rows, dtype=jnp.int32)).reshape(-1)
    opens = jnp.max(jnp.where(place[:, None] >= ends[None, :], ends[None, :], 0), axis=1)
    lower = jnp.maximum(opens, place - (W - 1)) - base
    least = lower.reshape(-1, TILE)[:, 0] // TILE
    meta = jnp.concatenate([tp_index[None].astype(jnp.int32), least])
    lower = lower[None, :]

    zeros = jnp.zeros_like(query_bias)
    qkv = low(
        (matmul(inputs_rows, qkv_full) + jnp.concatenate([query_bias, zeros, value_bias]))
        * jnp.concatenate([zeros + 0.125, zeros + 1.0, zeros + 1.0])
    )
    old_kv = low(matmul(old_rows, qkv_full[:, width:]) + jnp.concatenate([zeros, value_bias]))
    small_near = gather_tree(small_far, near_steps, None, qkv)
    qkv = after(qkv, out_near, small_near)
    mixed, mixed_t, self_lse = attend(width, qkv, qkv, meta, lower, old_kv)
    out_full = gather_tree(out_near, ctx_steps, qkv_full, mixed)
    mkv_full = gather_tree(small_near[:, : 2 * width], ctx_steps, None, mixed)
    up_far = gather_tree(up_own, far_steps, small_near, mixed)
    mixed = after(mixed, mkv_full, up_far)
    attn_part = scatter_tree(
        lambda s: contract("rk,dk->rd", mixed[s], out_full), rows, row_steps[-1:]
    )

    mkv_own = low(
        matmul(states, after(mkv_full, attn_part)) + jnp.concatenate([zeros, memory_vbias])
    )

    def weight_terms(*pairs):
        def make(s):
            return jnp.concatenate(
                [contract("rd,rk->dk", left[:, s], right) for left, right in pairs], axis=1
            )

        return make

    model = share.shape[1]

    attn_share = scatter_more(attn_part, row_steps[:-1])
    first, normed_one, rstd_one = layer_norm(
        wide(share) + attn_share + out_bias, gain_self, shift_self
    )
    up_near = gather_tree(up_far, near_steps, mixed, attn_part)
    down_far = gather_tree(down_own, far_steps, mixed, attn_part)
    mkv = gather_tree(mkv_own, ctx_steps)
    small_full = gather_tree(small_near[:, 2 * width :], ctx_steps, mixed, attn_part)
    first_low = after(low(first), up_near, down_far, mkv, small_full)
    mquery_full, mout_full = small_full[:, :width], small_full[:, width:]
    half_rows = gather_tree(first_low, row_steps[:-1])
    down_near = gather_tree(down_far, near_steps, first_low, half_rows)
    up_ready = gather_tree(split(up_near, 1, 2)[0], ctx_steps, first_low, half_rows)
    half_rows = after(half_rows, down_near, up_ready)
    first_rows = gather_tree(half_rows, row_steps[-1:])
    mquery = low((matmul(first_rows, mquery_full) + memory_qbias) * 0.125)
    cross_mixed, cross_mixed_t, cross_lse = attend(width, mquery, mkv)
    up_parts = [
        up_ready,
        gather_tree(split(up_near, 1, 2)[1], ctx_steps, half_rows, cross_mixed),
    ]
    cross_mixed = after(cross_mixed, up_parts[1])
    cross_part = scatter_tree(
        lambda s: contract("rk,dk->rd", cross_mixed[s], mout_full), rows, row_steps[-1:]
    )
    cross_share = scatter_more(cross_part, row_steps[:-1])
    second, normed_two, rstd_two = layer_norm(
        first + cross_share + memory_obias, gain_memory, shift_memory
    )
    down_ready = gather_tree(split(down_near, 1, 2)[0], ctx_steps, cross_mixed, cross_part)
    second_low = after(low(second), down_ready)
    half_second = gather_tree(second_low, row_steps[:-1])
    down_parts = [
        down_ready,
        gather_tree(split(down_near, 1, 2)[1], ctx_steps, second_low, half_second),
    ]
    second_rows = gather_tree(after(half_second, down_parts[1]), row_steps[-1:])
    up_full = lax.optimization_barrier(
        jnp.concatenate([after(up_parts[0], cross_part), up_parts[1]], axis=1)
    )
    act, slope = gelu_and_slope(matmul(second_rows, up_full) + up_bias)
    act_low, slope_low = low(act), low(slope)

    def dense_term(s):
        terms = [
            contract("rf,df->rd", a, part)
            for a, part in zip(split(act_low[s], 1, 2), down_parts, strict=True)
        ]
        return terms[0] + terms[1]

    dense_part = scatter_tree(dense_term, rows, row_steps[-1:])
    dense_share = scatter_more(dense_part, row_steps[:-1])
    down_full = lax.optimization_barrier(
        jnp.concatenate([after(down_parts[0], dense_part), down_parts[1]], axis=1)
    )
    result, normed_three, rstd_three = layer_norm(
        second + dense_share + down_bias, gain_dense, shift_dense
    )
    grad_three, gain_dense_grad, shift_dense_grad = norm_back(
        upstream, normed_three, rstd_three, gain_dense
    )
    dense_low = low(grad_three)
    dense_rows = gather_rows(dense_low)
    hidden_low = low(matmul(dense_rows, down_full) * wide(slope_low))
    second_share = scatter_rows(lambda s: contract("rf,df->rd", hidden_low[s], up_full))
    grad_two, gain_memory_grad, shift_memory_grad = norm_back(
        grad_three + second_share, normed_two, rstd_two, gain_memory
    )

    cross_low = low(grad_two)
    cross_rows = gather_rows(cross_low)
    down_part = scatter_tree(weight_terms((dense_rows, act_low)), model, ctx_steps, cross_rows)
    grad_cross_mixed = low(matmul(cross_rows, mout_full))
    mquery_back, mkv_sum = attend_back(
        width, "cross", mquery, grad_cross_mixed, cross_mixed_t, cross_lse, mkv
    )
    mquery_pre = mquery_back * 0.125
    down_near_grad = scatter_more(down_part, near_steps, None, mquery_pre)
    up_part = scatter_tree(
        weight_terms((second_rows, hidden_low)), model, ctx_steps, mquery_pre, cross_low
    )
    first_part = scatter_tree(
        lambda s: contract("rk,dk->rd", mquery_pre[s], mquery_full), rows, row_steps[-1:]
    )
    first_share = scatter_more(first_part, row_steps[:-1])
    grad_one, gain_self_grad, shift_self_grad = norm_back(
        grad_two + first_share, normed_one, rstd_one, gain_self
    )
    self_low = low(grad_one)
    self_rows = gather_rows(self_low)
    down_grads = scatter_more(down_near_grad, far_steps, first_part, self_low)
    up_near_grad = scatter_more(up_part, near_steps, first_part, self_low)
    up_grads = scatter_more(up_near_grad, far_steps, None, self_rows)
    mkv_back = after(mkv_sum, first_part)
    mkv_low = low(scatter_tree(lambda s: mkv_back[s], mkv_back.shape[0], ctx_steps))
    encoded_grad = scatter_tree(
        lambda s: contract("ek,dk->ed", mkv_low[s], mkv_full), states.shape[0], row_steps
    )
    small_part = scatter_tree(
        weight_terms((states, mkv_low), (first_rows, mquery_pre), (cross_rows, cross_mixed)),
        model,
        ctx_steps,
        self_rows,
    )
    grad_self = after(low(matmul(self_rows, out_full)), small_part)

    query_start, old_back = attend_back(
        width, "old", qkv, grad_self, mixed_t, self_lse, old_kv, meta, lower
    )
    out_terms = weight_terms((self_rows, mixed))
    out_far = low(out_terms(slice(model // 2, model)))
    back = shift(after(old_back, out_far), "ctx", -1)
    out_part = scatter_tree(out_terms, model, ctx_steps, query_start, None, out_far)
    small_near_grads = scatter_more(small_part, near_steps, None, old_back)
    grad_self_later = after(grad_self, small_near_grads, query_start, out_part)
    query_back, kv_back = attend_back(
        width, "own", qkv, grad_self_later, mixed_t, self_lse, None, meta, lower, query_start
    )
    out_near_grads = scatter_more(out_part, near_steps, None, query_back)
    query_pre = query_back * 0.125
    small_grads = scatter_more(small_near_grads, far_steps, None, query_pre)
    small_grads = with_layout_constraint(small_grads, Layout((0, 1)))
    own_back = jnp.concatenate([query_pre, kv_back], axis=1)

    def qkv_terms(s):
        own = contract("rd,rk->dk", inputs_rows[:, s], own_back)
        old = contract("rd,rk->dk", old_rows[:, s], old_back)
        return own + jnp.pad(old, ((0, 0), (width, 0)))

    kv_all = low(wide(kv_back) + wide(back))

    def inputs_term(s):
        term = contract("rk,dk->rd", query_pre[s], qkv_full[:, :width])
        return term + contract("rk,dk->rd", kv_all[s], qkv_full[:, width:])

    inputs_part = scatter_tree(inputs_term, rows, row_steps[-1:])
    inputs_grad = grad_one + scatter_more(inputs_part, row_steps[:-1])
    sent = low(inputs_part[inputs_part.shape[0] // 2 :])
    qkv_grads = scatter_more(
        scatter_tree(qkv_terms, model, ctx_steps, sent), weight_steps[: -len(ctx_steps)]
    )
    out_grads = scatter_more(out_near_grads, far_steps, None, sent)

    everywhere = jnp.stack(
        [
            column_sum(self_low),
            column_sum(cross_low),
            column_sum(dense_low),
            gain_self_grad,
            shift_self_grad,
            gain_memory_grad,
            shift_memory_grad,
            gain_dense_grad,
            shift_dense_grad,
        ]
    )
    everywhere = all_sum(turned_back(everywhere, 1), row_steps)
    by_heads = jnp.concatenate(
        [
            column_sum(query_pre),
            column_sum(kv_back[:, width:]) + column_sum(old_back[:, width:]),
            column_sum(mquery_pre),
            column_sum(mkv_low[:, width:]),
            column_sum(hidden_low),
        ]
    )
    lanes = 128
    sums = all_sum(
        after(
            jnp.concatenate([everywhere.reshape(-1, lanes), by_heads.reshape(-1, lanes)], axis=0),
            sent,
        ),
        weight_steps,
    )
    cut = everywhere.size // lanes
    totals = sums[:cut].reshape(everywhere.shape)
    head_totals = sums[cut:].reshape(-1)
    return (
        turned_back(low(result), 1)[None],
        turned_back(inputs_grad, 1)[None],
        turned_back(encoded_grad, 1)[None],
        qkv_grads[:, :width],
        qkv_grads[:, width : 2 * width],
        qkv_grads[:, 2 * width :],
        out_grads.T,
        small_grads[:, 2 * width : 3 * width],
        small_grads[:, :width],
        small_grads[:, width : 2 * width],
        small_grads[:, 3 * width :].T,
        up_grads,
        down_grads.T,
        head_totals[:width],
        head_totals[width : 2 * width],
        head_totals[2 * width : 3 * width],
        head_totals[3 * width : 4 * width],
        head_totals[4 * width :],
        totals[0],
        totals[1],
        totals[2],
        totals[3],
        totals[4],
        totals[5],
        totals[6],
        totals[7],
        totals[8],
    )


def solution(mesh):
    placed = (
        P("shard", ("ctx", "tp"), None),
        P("shard", "ctx", None),
        P("shard", None),
        P("shard", ("ctx", "tp"), None),
        P("shard", "tp"),
        P("shard", "tp"),
        P("shard", "tp"),
        P("tp", "shard"),
        P("shard", "tp"),
        P("shard", "tp"),
        P("shard", "tp"),
        P("tp", "shard"),
        P("shard", "tp"),
        P("tp", "shard"),
        P("tp"),
        P("tp"),
        P("tp"),
        P("tp"),
        P("tp"),
        P(),
        P(),
        P(),
        P(),
        P(),
        P(),
        P(),
        P(),
        P(),
    )
    return jax.shard_map(
        per_device,
        mesh=mesh,
        in_specs=placed,
        out_specs=(
            P("shard", ("ctx", "tp"), None),
            P("shard", ("ctx", "tp"), None),
            P("shard", ("ctx", "tp"), None),
            P(("shard", "ctx"), "tp"),
            P(("shard", "ctx"), "tp"),
            P(("shard", "ctx"), "tp"),
            P("tp", ("shard", "ctx")),
            P(("shard", "ctx"), "tp"),
            P(("shard", "ctx"), "tp"),
            P(("shard", "ctx"), "tp"),
            P("tp", ("shard", "ctx")),
            P(("shard", "ctx"), "tp"),
            P("tp", ("shard", "ctx")),
            P("tp"),
            P("tp"),
            P("tp"),
            P("tp"),
            P("tp"),
            P(),
            P(),
            P(),
            P(),
            P(),
            P(),
            P(),
            P(),
            P(),
        ),
        check_vma=False,
    )
```

```python
from functools import partial

import jax
import jax.numpy as jnp
from jax import lax
from jax.experimental import pallas as pl
from jax.experimental.layout import Layout, with_layout_constraint
from jax.experimental.pallas import tpu as pltpu
from jax.sharding import PartitionSpec as P

HDIM = 64
W = 1024
TILE = 256


EPSILON = 1e-05
NEGATIVE = -1e30
VMEM = 32 * 1024 * 1024


def matmul(left, right):
    return jnp.dot(left, right, preferred_element_type=jnp.float32)


def contract(form, left, right):
    return jnp.einsum(form, left, right, preferred_element_type=jnp.float32)


def low(value):
    return value.astype(jnp.bfloat16)


def wide(value):
    return value.astype(jnp.float32)


def swap(array, axis, bit):
    return lax.ppermute(array, axis, [(i, i ^ bit) for i in range(lax.axis_size(axis))])


def shift(array, axis, by):
    count = lax.axis_size(axis)
    pairs = [(i, i + by) for i in range(count) if 0 <= i + by < count]
    return lax.ppermute(array, axis, pairs)


def steps_of(*axes):
    steps = []
    for axis in axes:
        bit = lax.axis_size(axis) // 2
        while bit:
            steps.append((axis, bit))
            bit //= 2
    return steps


def after(value, *others):
    others = [other for other in others if other is not None]
    return lax.optimization_barrier((value, *others))[0] if others else value


def gather_tree(array, steps, start=None, used=None):
    for n, (axis, bit) in enumerate(steps):
        arrived = swap(after(array, start if n == 0 else None), axis, bit)
        array = jnp.concatenate([after(array, used if n == len(steps) - 1 else None), arrived])
    return array


def scatter_more(total, steps, start=None, used=None):
    for n, (axis, bit) in enumerate(reversed(steps)):
        half = total.shape[0] // 2
        arrived = swap(after(low(total[half:]), start if n == 0 else None), axis, bit)
        kept = after(total[:half], used if n == len(steps) - 1 else None)
        total = kept + wide(arrived)
    return total


def scatter_tree(make, size, steps, used=None, start=None, far=None):
    axis, bit = steps[-1]
    half = size // 2
    if far is None:
        far = low(make(slice(half, size)))
    arrived = swap(after(far, start), axis, bit)
    total = after(make(slice(0, half)), used) + wide(arrived)
    return scatter_more(total, steps[:-1])


def all_sum(value, steps):
    for axis, bit in steps:
        value = value + swap(value, axis, bit)
    return value


def flat_bit(step, axes):
    axis, bit = step
    for other in axes[axes.index(axis) + 1 :]:
        bit = bit * lax.axis_size(other)
    return bit


def masks_of(axes, steps):
    masks = [0]
    for step in steps:
        masks = masks + [m | flat_bit(step, axes) for m in masks]
    return masks


def cross_over(blocks, axes):
    index = lax.axis_index(axes)
    bit = 1
    while bit < len(blocks):
        odd = (index & bit) != 0
        blocks = [jnp.where(odd, blocks[m ^ bit], blocks[m]) for m in range(len(blocks))]
        bit *= 2
    return blocks


def split(array, dim, count):
    size = array.shape[dim] // count
    return [lax.slice_in_dim(array, m * size, (m + 1) * size, axis=dim) for m in range(count)]


def to_tree(array, dim, axes, steps):
    masks = masks_of(axes, steps)
    blocks = cross_over(split(array, dim, len(masks)), axes)
    return jnp.concatenate([blocks[m] for m in masks], axis=dim)


def from_tree(array, dim, axes, steps):
    masks = masks_of(axes, steps)
    blocks = split(array, dim, len(masks))
    blocks = cross_over([blocks[masks.index(m)] for m in range(len(masks))], axes)
    return jnp.concatenate(blocks, axis=dim)


def in_tree(block, bits):
    return sum(((block >> k) & 1) << (bits - 1 - k) for k in range(bits))


def stack_heads(value, heads, turned):
    feature = lax.broadcasted_iota(jnp.int32, value.shape, 0 if turned else 1) // HDIM
    zero = jnp.zeros_like(value)
    parts = [jnp.where(feature == h, value, zero) for h in range(heads)]
    return jnp.concatenate(parts, axis=1 if turned else 0)


def allowed_in(lower, query, key_start, count):
    key = key_start + lax.broadcasted_iota(jnp.int32, (count, lower.shape[1]), 0)
    return (key >= lower) & (key <= query)


def along_heads(row, heads):
    return jnp.concatenate([row] * heads, axis=1)


def tile_of(ref, index, count, columns=None):
    rows = pl.ds(pl.multiple_of(index * count, count), count)
    return ref[rows, :] if columns is None else ref[rows, columns]


def lanes_of(index, count):
    return pl.ds(pl.multiple_of(index * count, count), count)


def attend_kernel(width, masked, *refs):
    if masked:
        meta, lower_ref, source_ref, old_ref, mixed_ref, mixed_t_ref, lse_ref, acc_ref = refs
        query_ref, first = source_ref, width
    else:
        query_ref, source_ref, mixed_ref, mixed_t_ref, lse_ref, acc_ref = refs
        first = 0
    heads, count = width // HDIM, TILE
    steps = mixed_ref.shape[0] // count
    bits = steps.bit_length() - 1

    @pl.loop(0, steps)
    def _(step):
        stacked = stack_heads(tile_of(query_ref, step, count, slice(0, width)).T, heads, True)
        acc_ref[...] = jnp.zeros_like(acc_ref)
        if masked:
            tile = in_tree(step, bits) ^ meta[0]
            lower = along_heads(lower_ref[:, lanes_of(step, count)], heads)
            place_of = tile * count + lax.broadcasted_iota(jnp.int32, (1, count), 1)
            place_of = along_heads(place_of, heads)

        def add(carry, ref, column, place, key_tile, masking, size=count):
            keys = tile_of(ref, place, size, slice(column, column + width))
            values_t = tile_of(ref, place, size, slice(column + width, column + 2 * width)).T
            top, total = carry
            scores = matmul(keys, stacked)
            if masking:
                ok = allowed_in(lower, place_of, key_tile * count, count)
                scores = jnp.where(ok, scores, NEGATIVE)
            higher = jnp.maximum(top, jnp.max(scores, axis=0, keepdims=True))
            expo = jnp.exp(scores - higher)
            scale = jnp.exp(top - higher)
            total = total * scale + jnp.sum(expo, axis=0, keepdims=True)
            expo = low(expo)
            for h in range(heads):
                part, lanes = slice(h * HDIM, (h + 1) * HDIM), slice(h * count, (h + 1) * count)
                acc_ref[part, :] = acc_ref[part, :] * scale[:, lanes] + matmul(
                    values_t[part, :], expo[:, lanes]
                )
            return higher, total

        carry = (
            jnp.full((1, heads * count), NEGATIVE, jnp.float32),
            jnp.zeros((1, heads * count), jnp.float32),
        )
        if masked:
            least = meta[1 + step]
            here = lambda n, c: add(
                c, source_ref, first, in_tree((tile - n) ^ meta[0], bits), tile - n, True
            )
            carry = lax.fori_loop(0, tile - jnp.maximum(least, 0) + 1, here, carry)
            before = lambda n, c: add(
                c, old_ref, 0, in_tree((n + steps) ^ meta[0], bits), n, True
            )
            carry = lax.fori_loop(least, 0, before, carry)
        else:
            every = lambda n, c: add(c, source_ref, first, n, n, False, 2 * count)
            carry = lax.fori_loop(0, source_ref.shape[0] // (2 * count), every, carry)
        top, total = carry
        lse = top + jnp.log(total)
        whole = lanes_of(step, count)
        for h in range(heads):
            part, lanes = slice(h * HDIM, (h + 1) * HDIM), slice(h * count, (h + 1) * count)
            acc_ref[part, :] = acc_ref[part, :] / total[:, lanes]
            lse_ref[h : h + 1, whole] = lse[:, lanes]
        mixed_t_ref[:, whole] = acc_ref[...]
        mixed_ref[whole, :] = low(acc_ref[...].T)


def attend_back_kernel(width, kind, *refs):
    refs = list(refs)
    masked, old = kind != "cross", kind == "old"
    if masked:
        meta, lower_ref = refs.pop(0), refs.pop(0)
    start_ref = refs.pop(0) if kind == "own" else None
    query_ref = refs.pop(0)
    grad_ref, mixed_t_ref, lse_ref = refs[:3]
    refs = refs[3:]
    source_ref = query_ref if kind == "own" else refs.pop(0)
    first = width if kind == "own" else 0
    grad_query_ref, grad_kv_ref, keys_acc, values_acc, query_acc = refs
    heads, count = width // HDIM, TILE
    steps = grad_ref.shape[0] // count
    bits = steps.bit_length() - 1
    keys_acc[...] = jnp.zeros_like(keys_acc)
    values_acc[...] = jnp.zeros_like(values_acc)

    def of_queries(step):
        whole = lanes_of(step, count)
        query = tile_of(query_ref, step, count, slice(0, width))
        grad = tile_of(grad_ref, step, count)
        grad_t = grad.T
        stacked = stack_heads(query, heads, False)
        stacked_t = stack_heads(query.T, heads, True)
        stacked_grad = stack_heads(grad, heads, False)
        stacked_grad_t = stack_heads(grad_t, heads, True)
        weighed = wide(grad_t) * mixed_t_ref[:, whole]
        lse = jnp.concatenate([lse_ref[h : h + 1, whole] for h in range(heads)], axis=1)
        inner = jnp.concatenate(
            [
                jnp.sum(weighed[h * HDIM : (h + 1) * HDIM, :], axis=0, keepdims=True)
                for h in range(heads)
            ],
            axis=1,
        )
        if masked:
            tile = in_tree(step, bits) ^ meta[0]
            lower = along_heads(lower_ref[:, whole], heads)
            place_of = tile * count + lax.broadcasted_iota(jnp.int32, (1, count), 1)
            place_of = along_heads(place_of, heads)

        def add(place, key_tile, size=count):
            rows = pl.ds(pl.multiple_of(place * size, size), size)
            keys = source_ref[rows, first : first + width]
            values = source_ref[rows, first + width : first + 2 * width]
            keys_t = keys.T
            probs = jnp.exp(matmul(keys, stacked_t) - lse)
            if masked:
                ok = allowed_in(lower, place_of, key_tile * count, count)
                probs = jnp.where(ok, probs, 0.0)
            slopes = low(probs * (matmul(values, stacked_grad_t) - inner))
            values_acc[rows, :] += matmul(low(probs), stacked_grad)
            keys_acc[rows, :] += matmul(slopes, stacked)
            for h in range(heads):
                part, lanes = slice(h * HDIM, (h + 1) * HDIM), slice(h * count, (h + 1) * count)
                query_acc[part, :] += matmul(keys_t[part, :], slopes[:, lanes])

        if not masked:
            pl.loop(0, source_ref.shape[0] // (2 * count))(lambda n: add(n, n, 2 * count))
        elif old:
            pl.loop(meta[1 + step], 0)(lambda n: add(in_tree((n + steps) ^ meta[0], bits), n))
        else:
            pl.loop(jnp.maximum(meta[1 + step], 0), tile + 1)(
                lambda n: add(in_tree(n ^ meta[0], bits), n)
            )

    @pl.loop(0, steps)
    def _(step):
        whole = lanes_of(step, count)
        if start_ref is None:
            query_acc[...] = jnp.zeros_like(query_acc)
        else:
            query_acc[...] = start_ref[:, whole]
        if old:
            pl.when(meta[1 + step] < 0)(lambda: of_queries(step))
            grad_query_ref[:, whole] = query_acc[...]
        else:
            of_queries(step)
            grad_query_ref[whole, :] = low(query_acc[...].T)

    grad_kv_ref[:, :width] = keys_acc[...].astype(grad_kv_ref.dtype)
    grad_kv_ref[:, width:] = values_acc[...].astype(grad_kv_ref.dtype)


IN_VMEM = pl.BlockSpec(memory_space=pltpu.VMEM)
IN_SMEM = pl.BlockSpec(memory_space=pltpu.SMEM)


def attend(width, query, source, meta=None, lower=None, old=None):
    rows = query.shape[0]
    heads = width // HDIM
    masked = old is not None
    inputs = [meta, lower, source, old] if masked else [query, source]
    specs = [IN_SMEM if masked else IN_VMEM] + [IN_VMEM] * (len(inputs) - 1)
    pairs = rows * source.shape[0] * width
    return pl.pallas_call(
        partial(attend_kernel, width, masked),
        in_specs=specs,
        out_specs=[IN_VMEM] * 3,
        out_shape=[
            jax.ShapeDtypeStruct((rows, width), jnp.bfloat16),
            jax.ShapeDtypeStruct((width, rows), jnp.float32),
            jax.ShapeDtypeStruct((heads, rows), jnp.float32),
        ],
        scratch_shapes=[pltpu.VMEM((width, TILE), jnp.float32)],
        compiler_params=pltpu.CompilerParams(vmem_limit_bytes=VMEM),
        cost_estimate=pl.CostEstimate(
            flops=48 * pairs, bytes_accessed=8 * rows * width, transcendentals=0
        ),
    )(*inputs)


def attend_back(width, kind, query, grad, mixed_t, lse, source=None, meta=None, lower=None, start=None):
    rows = grad.shape[0]
    inputs = [] if kind == "cross" else [meta, lower]
    inputs += [start] if kind == "own" else []
    inputs += [query, grad, mixed_t, lse] + ([] if kind == "own" else [source])
    specs = [IN_VMEM] * len(inputs)
    if kind != "cross":
        specs[0] = IN_SMEM
    count = (query if kind == "own" else source).shape[0]
    pairs = rows * count * width
    return pl.pallas_call(
        partial(attend_back_kernel, width, kind),
        in_specs=specs,
        out_specs=[IN_VMEM] * 2,
        out_shape=[
            jax.ShapeDtypeStruct((width, rows), jnp.float32)
            if kind == "old"
            else jax.ShapeDtypeStruct((rows, width), jnp.bfloat16),
            jax.ShapeDtypeStruct(
                (count, 2 * width), jnp.float32 if kind == "cross" else jnp.bfloat16
            ),
        ],
        scratch_shapes=[
            pltpu.VMEM((count, width), jnp.float32),
            pltpu.VMEM((count, width), jnp.float32),
            pltpu.VMEM((width, TILE), jnp.float32),
        ],
        compiler_params=pltpu.CompilerParams(vmem_limit_bytes=VMEM),
        cost_estimate=pl.CostEstimate(
            flops=64 * pairs, bytes_accessed=16 * rows * width, transcendentals=0
        ),
    )(*inputs)


def layer_norm(value, gain, shift_by):
    centre = value - jnp.mean(value, axis=-1, keepdims=True)
    rstd = lax.rsqrt(jnp.mean(centre * centre, axis=-1, keepdims=True) + EPSILON)
    normed = centre * rstd
    return (normed * gain + shift_by, normed, rstd)


def norm_back(grad_out, normed, rstd, gain):
    scaled = grad_out * gain
    inner = scaled - jnp.mean(scaled, axis=-1, keepdims=True)
    inner = inner - normed * jnp.mean(scaled * normed, axis=-1, keepdims=True)
    return (rstd * inner, jnp.sum(grad_out * normed, axis=0), jnp.sum(grad_out, axis=0))


def gelu_and_slope(value):
    phi = 0.5 * (1.0 + lax.erf(value * 0.7071067811865476))
    bell = jnp.exp(-0.5 * value * value) * 0.3989422804014327
    return value * phi, phi + value * bell


def column_sum(value):
    return jnp.sum(wide(value), axis=0)


def per_device(
    inputs,
    encoded,
    doc_lengths,
    cotangent,
    query_weight,
    key_weight,
    value_weight,
    out_weight,
    memory_query,
    memory_key,
    memory_value,
    memory_out,
    up_weight,
    down_weight,
    query_bias,
    value_bias,
    memory_qbias,
    memory_vbias,
    up_bias,
    out_bias,
    memory_obias,
    down_bias,
    gain_self,
    shift_self,
    gain_memory,
    shift_memory,
    gain_dense,
    shift_dense,
):
    tp_index = lax.axis_index("tp")
    share_rows = inputs.shape[1]
    rows = share_rows * lax.axis_size("tp")
    width = query_weight.shape[1]
    base = lax.axis_index("ctx") * rows
    row_steps = steps_of("tp")
    weight_steps = steps_of("shard", "ctx")
    features = ("shard", "ctx")

    def turned(array, dim):
        return to_tree(array, dim, features, weight_steps)

    def turned_back(array, dim):
        return from_tree(array, dim, features, weight_steps)

    def gather_rows(piece):
        return gather_tree(piece, row_steps)

    def scatter_rows(make):
        return scatter_tree(make, rows, row_steps)

    def own_half(weight):
        part = weight.shape[0] // lax.axis_size("ctx")
        return lax.dynamic_slice_in_dim(weight, lax.axis_index("ctx") * part, part, 0)

    ctx_steps = steps_of("ctx")
    far_steps, near_steps = steps_of("shard")[:-1], steps_of("shard")[-1:]
    share = turned(inputs[0], 1)
    old_share = turned(shift(inputs[0], "ctx", 1), 1)
    inputs_rows = lax.optimization_barrier(gather_rows(share))
    old_rows = lax.optimization_barrier(gather_rows(old_share))
    qkv_own = own_half(jnp.concatenate([query_weight, key_weight, value_weight], axis=1))
    qkv_far = gather_tree(qkv_own, far_steps)
    qkv_near = gather_tree(qkv_far, near_steps)
    qkv_full = gather_tree(qkv_near, ctx_steps)
    out_far = gather_tree(own_half(out_weight.T), far_steps, qkv_far)
    out_near = gather_tree(out_far, near_steps, qkv_near)
    small_own = jnp.concatenate([memory_key, memory_value, memory_query, memory_out.T], axis=1)
    small_own = with_layout_constraint(small_own, Layout((0, 1)))
    small_far = gather_tree(own_half(small_own), far_steps, qkv_near)
    up_own = own_half(up_weight)
    down_own = own_half(down_weight.T)
    states = to_tree(turned(encoded[0], 1), 0, ("tp",), row_steps)
    vectors = turned(
        jnp.stack(
            [
                out_bias,
                memory_obias,
                down_bias,
                gain_self,
                shift_self,
                gain_memory,
                shift_memory,
                gain_dense,
                shift_dense,
            ]
        ),
        1,
    )
    (
        out_bias,
        memory_obias,
        down_bias,
        gain_self,
        shift_self,
        gain_memory,
        shift_memory,
        gain_dense,
        shift_dense,
    ) = [vectors[i] for i in range(9)]
    upstream = wide(turned(cotangent[0], 1))

    ends = jnp.cumsum(doc_lengths[0], dtype=jnp.int32)
    masks = jnp.asarray(masks_of(("tp",), row_steps), jnp.int32)
    starts = (masks ^ tp_index) * share_rows
    place = base + (starts[:, None] + jnp.arange(share_rows, dtype=jnp.int32)).reshape(-1)
    opens = jnp.max(jnp.where(place[:, None] >= ends[None, :], ends[None, :], 0), axis=1)
    lower = jnp.maximum(opens, place - (W - 1)) - base
    least = lower.reshape(-1, TILE)[:, 0] // TILE
    meta = jnp.concatenate([tp_index[None].astype(jnp.int32), least])
    lower = lower[None, :]

    zeros = jnp.zeros_like(query_bias)
    qkv = low(
        (matmul(inputs_rows, qkv_full) + jnp.concatenate([query_bias, zeros, value_bias]))
        * jnp.concatenate([zeros + 0.125, zeros + 1.0, zeros + 1.0])
    )
    old_kv = low(matmul(old_rows, qkv_full[:, width:]) + jnp.concatenate([zeros, value_bias]))
    small_near = gather_tree(small_far, near_steps, None, qkv)
    qkv = after(qkv, out_near, small_near)
    mixed, mixed_t, self_lse = attend(width, qkv, qkv, meta, lower, old_kv)
    out_full = gather_tree(out_near, ctx_steps, qkv_full, mixed)
    mkv_full = gather_tree(small_near[:, : 2 * width], ctx_steps, None, mixed)
    up_far = gather_tree(up_own, far_steps, small_near, mixed)
    mixed = after(mixed, mkv_full, up_far)
    attn_part = scatter_tree(
        lambda s: contract("rk,dk->rd", mixed[s], out_full), rows, row_steps[-1:]
    )

    mkv_own = low(
        matmul(states, after(mkv_full, attn_part)) + jnp.concatenate([zeros, memory_vbias])
    )

    def weight_terms(*pairs):
        def make(s):
            return jnp.concatenate(
                [contract("rd,rk->dk", left[:, s], right) for left, right in pairs], axis=1
            )

        return make

    model = share.shape[1]

    attn_share = scatter_more(attn_part, row_steps[:-1])
    first, normed_one, rstd_one = layer_norm(
        wide(share) + attn_share + out_bias, gain_self, shift_self
    )
    up_near = gather_tree(up_far, near_steps, mixed, attn_part)
    down_far = gather_tree(down_own, far_steps, mixed, attn_part)
    mkv = gather_tree(mkv_own, ctx_steps)
    small_full = gather_tree(small_near[:, 2 * width :], ctx_steps, mixed, attn_part)
    first_low = after(low(first), up_near, down_far, mkv, small_full)
    mquery_full, mout_full = small_full[:, :width], small_full[:, width:]
    half_rows = gather_tree(first_low, row_steps[:-1])
    down_near = gather_tree(down_far, near_steps, first_low, half_rows)
    up_ready = gather_tree(split(up_near, 1, 2)[0], ctx_steps, first_low, half_rows)
    half_rows = after(half_rows, down_near, up_ready)
    first_rows = gather_tree(half_rows, row_steps[-1:])
    mquery = low((matmul(first_rows, mquery_full) + memory_qbias) * 0.125)
    cross_mixed, cross_mixed_t, cross_lse = attend(width, mquery, mkv)
    up_parts = [
        up_ready,
        gather_tree(split(up_near, 1, 2)[1], ctx_steps, half_rows, cross_mixed),
    ]
    cross_mixed = after(cross_mixed, up_parts[1])
    cross_part = scatter_tree(
        lambda s: contract("rk,dk->rd", cross_mixed[s], mout_full), rows, row_steps[-1:]
    )
    cross_share = scatter_more(cross_part, row_steps[:-1])
    second, normed_two, rstd_two = layer_norm(
        first + cross_share + memory_obias, gain_memory, shift_memory
    )
    down_ready = gather_tree(split(down_near, 1, 2)[0], ctx_steps, cross_mixed, cross_part)
    second_low = after(low(second), down_ready)
    half_second = gather_tree(second_low, row_steps[:-1])
    down_parts = [
        down_ready,
        gather_tree(split(down_near, 1, 2)[1], ctx_steps, second_low, half_second),
    ]
    second_rows = gather_tree(after(half_second, down_parts[1]), row_steps[-1:])
    up_full = lax.optimization_barrier(
        jnp.concatenate([after(up_parts[0], cross_part), up_parts[1]], axis=1)
    )
    act, slope = gelu_and_slope(matmul(second_rows, up_full) + up_bias)
    act_low, slope_low = low(act), low(slope)

    def dense_term(s):
        terms = [
            contract("rf,df->rd", a, part)
            for a, part in zip(split(act_low[s], 1, 2), down_parts, strict=True)
        ]
        return terms[0] + terms[1]

    dense_part = scatter_tree(dense_term, rows, row_steps[-1:])
    dense_share = scatter_more(dense_part, row_steps[:-1])
    down_full = lax.optimization_barrier(
        jnp.concatenate([after(down_parts[0], dense_part), down_parts[1]], axis=1)
    )
    result, normed_three, rstd_three = layer_norm(
        second + dense_share + down_bias, gain_dense, shift_dense
    )
    grad_three, gain_dense_grad, shift_dense_grad = norm_back(
        upstream, normed_three, rstd_three, gain_dense
    )
    dense_low = low(grad_three)
    dense_rows = gather_rows(dense_low)
    down_terms = weight_terms((dense_rows, act_low))
    down_far_term = low(down_terms(slice(model // 2, model)))
    hidden_low = low(matmul(dense_rows, down_full) * wide(slope_low))
    hidden_low = after(hidden_low, down_far_term)
    second_share = scatter_rows(lambda s: contract("rf,df->rd", hidden_low[s], up_full))
    grad_two, gain_memory_grad, shift_memory_grad = norm_back(
        grad_three + second_share, normed_two, rstd_two, gain_memory
    )

    cross_low = low(grad_two)
    cross_rows = gather_rows(cross_low)
    down_part = scatter_tree(down_terms, model, ctx_steps, cross_low, None, down_far_term)
    cross_rows = after(cross_rows, down_part)
    grad_cross_mixed = low(matmul(cross_rows, mout_full))
    mquery_back, mkv_sum = attend_back(
        width, "cross", mquery, grad_cross_mixed, cross_mixed_t, cross_lse, mkv
    )
    mquery_pre = mquery_back * 0.125
    down_near_grad = scatter_more(down_part, near_steps, None, mquery_pre)
    up_part = scatter_tree(
        weight_terms((second_rows, hidden_low)), model, ctx_steps, mquery_pre, cross_low
    )
    first_part = scatter_tree(
        lambda s: contract("rk,dk->rd", mquery_pre[s], mquery_full), rows, row_steps[-1:]
    )
    first_share = scatter_more(first_part, row_steps[:-1])
    grad_one, gain_self_grad, shift_self_grad = norm_back(
        grad_two + first_share, normed_one, rstd_one, gain_self
    )
    self_low = low(grad_one)
    self_rows = gather_rows(self_low)
    down_grads = scatter_more(down_near_grad, far_steps, first_part, self_low)
    up_near_grad = scatter_more(up_part, near_steps, first_part, self_low)
    up_grads = scatter_more(up_near_grad, far_steps, None, self_rows)
    mkv_back = after(mkv_sum, first_part)
    mkv_low = low(scatter_tree(lambda s: mkv_back[s], mkv_back.shape[0], ctx_steps))
    encoded_grad = scatter_tree(
        lambda s: contract("ek,dk->ed", mkv_low[s], mkv_full), states.shape[0], row_steps
    )
    small_part = scatter_tree(
        weight_terms((states, mkv_low), (first_rows, mquery_pre), (cross_rows, cross_mixed)),
        model,
        ctx_steps,
        self_rows,
    )
    grad_self = after(low(matmul(self_rows, out_full)), small_part)

    query_start, old_back = attend_back(
        width, "old", qkv, grad_self, mixed_t, self_lse, old_kv, meta, lower
    )
    out_terms = weight_terms((self_rows, mixed))
    out_far = low(out_terms(slice(model // 2, model)))
    back = shift(after(old_back, out_far), "ctx", -1)
    out_part = scatter_tree(out_terms, model, ctx_steps, query_start, None, out_far)
    small_near_grads = scatter_more(small_part, near_steps, None, old_back)
    grad_self_later = after(grad_self, small_near_grads, query_start, out_part)
    query_back, kv_back = attend_back(
        width, "own", qkv, grad_self_later, mixed_t, self_lse, None, meta, lower, query_start
    )
    out_near_grads = scatter_more(out_part, near_steps, None, query_back)
    query_pre = query_back * 0.125
    out_near_grads = scatter_more(out_part, near_steps, None, query_back)
    query_pre = query_back * 0.125
    small_grads = scatter_more(small_near_grads, far_steps, None, query_pre)
    small_grads = with_layout_constraint(small_grads, Layout((0, 1)))
    own_back = jnp.concatenate([query_pre, kv_back], axis=1)

    def qkv_terms(s):
        own = contract("rd,rk->dk", inputs_rows[:, s], own_back)
        old = contract("rd,rk->dk", old_rows[:, s], old_back)
        return own + jnp.pad(old, ((0, 0), (width, 0)))

    kv_all = low(wide(kv_back) + wide(back))

    def inputs_term(s):
        term = contract("rk,dk->rd", query_pre[s], qkv_full[:, :width])
        return term + contract("rk,dk->rd", kv_all[s], qkv_full[:, width:])

    inputs_part = scatter_tree(inputs_term, rows, row_steps[-1:])
    inputs_grad = grad_one + scatter_more(inputs_part, row_steps[:-1])
    sent = low(inputs_part[inputs_part.shape[0] // 2 :])
    qkv_grads = scatter_more(
        scatter_tree(qkv_terms, model, ctx_steps, sent), weight_steps[: -len(ctx_steps)]
    )
    out_grads = scatter_more(out_near_grads, far_steps, None, sent)

    everywhere = jnp.stack(
        [
            column_sum(self_low),
            column_sum(cross_low),
            column_sum(dense_low),
            gain_self_grad,
            shift_self_grad,
            gain_memory_grad,
            shift_memory_grad,
            gain_dense_grad,
            shift_dense_grad,
        ]
    )
    everywhere = all_sum(turned_back(everywhere, 1), row_steps)
    by_heads = jnp.concatenate(
        [
            column_sum(query_pre),
            column_sum(kv_back[:, width:]) + column_sum(old_back[:, width:]),
            column_sum(mquery_pre),
            column_sum(mkv_low[:, width:]),
            column_sum(hidden_low),
        ]
    )
    lanes = 128
    sums = all_sum(
        after(
            jnp.concatenate([everywhere.reshape(-1, lanes), by_heads.reshape(-1, lanes)], axis=0),
            sent,
        ),
        weight_steps,
    )
    cut = everywhere.size // lanes
    totals = sums[:cut].reshape(everywhere.shape)
    head_totals = sums[cut:].reshape(-1)
    return (
        turned_back(low(result), 1)[None],
        turned_back(inputs_grad, 1)[None],
        turned_back(encoded_grad, 1)[None],
        qkv_grads[:, :width],
        qkv_grads[:, width : 2 * width],
        qkv_grads[:, 2 * width :],
        out_grads.T,
        small_grads[:, 2 * width : 3 * width],
        small_grads[:, :width],
        small_grads[:, width : 2 * width],
        small_grads[:, 3 * width :].T,
        up_grads,
        down_grads.T,
        head_totals[:width],
        head_totals[width : 2 * width],
        head_totals[2 * width : 3 * width],
        head_totals[3 * width : 4 * width],
        head_totals[4 * width :],
        totals[0],
        totals[1],
        totals[2],
        totals[3],
        totals[4],
        totals[5],
        totals[6],
        totals[7],
        totals[8],
    )


def solution(mesh):
    placed = (
        P("shard", ("ctx", "tp"), None),
        P("shard", "ctx", None),
        P("shard", None),
        P("shard", ("ctx", "tp"), None),
        P("shard", "tp"),
        P("shard", "tp"),
        P("shard", "tp"),
        P("tp", "shard"),
        P("shard", "tp"),
        P("shard", "tp"),
        P("shard", "tp"),
        P("tp", "shard"),
        P("shard", "tp"),
        P("tp", "shard"),
        P("tp"),
        P("tp"),
        P("tp"),
        P("tp"),
        P("tp"),
        P(),
        P(),
        P(),
        P(),
        P(),
        P(),
        P(),
        P(),
        P(),
    )
    return jax.shard_map(
        per_device,
        mesh=mesh,
        in_specs=placed,
        out_specs=(
            P("shard", ("ctx", "tp"), None),
            P("shard", ("ctx", "tp"), None),
            P("shard", ("ctx", "tp"), None),
            P(("shard", "ctx"), "tp"),
            P(("shard", "ctx"), "tp"),
            P(("shard", "ctx"), "tp"),
            P("tp", ("shard", "ctx")),
            P(("shard", "ctx"), "tp"),
            P(("shard", "ctx"), "tp"),
            P(("shard", "ctx"), "tp"),
            P("tp", ("shard", "ctx")),
            P(("shard", "ctx"), "tp"),
            P("tp", ("shard", "ctx")),
            P("tp"),
            P("tp"),
            P("tp"),
            P("tp"),
            P("tp"),
            P(),
            P(),
            P(),
            P(),
            P(),
            P(),
            P(),
            P(),
            P(),
        ),
        check_vma=False,
    )
```
